256 devices in a mesh: fsdp: 64 (over y, z, core), tp: 4 (over x).
Axes of the slice: x: 4, y: 4, z: 8, core: 2. Of those that a mesh axis runs over, the one named last changes fastest.
Arguments:
- grad_q_up: bfloat16 [1536, 24576], P('tp', 'fsdp'), may hold values from -1 to 1
- grad_kv_down: bfloat16 [576, 7168], P('tp', 'fsdp'), may hold values from -1 to 1
- grad_kv_up: bfloat16 [512, 32768], P('tp', 'fsdp'), may hold values from -1 to 1
Outputs:
- step_q_up: bfloat16 [1536, 24576], P('tp', 'fsdp')
- step_kv_down: bfloat16 [576, 7168], P('tp', 'fsdp')
- step_kv_up: bfloat16 [512, 32768], P('tp', 'fsdp')
The draws below stay inside these ranges and needn't reach their ends.
All inputs are finite; a program needn't handle non-finite values.
Results may differ from the reference program's by a relative error of at most 0.012.
The reference program's roundings to bfloat16 on the way count: a program that leaves them out, or rounds other values in their place, can miss the bound.
Values may be sent and summed in bfloat16 or wider, within the bound.
No kernel may reach another device: no remote copies, remote signals or barrier semaphores. Data moves between devices by JAX's collectives and lax.ppermute only.
A program may use at most 64 MiB of HBM per device.

```python
import math
import jax
import jax.numpy as jnp
from jax import lax

M_QB = 1536
N_QB = 24576
M_KA = 576
N_KA = 7168
M_KB = 512
N_KB = 32768


def scaled(key, noise):
    rows, cols = noise.shape
    row_scale = jnp.exp(jax.random.uniform(jax.random.fold_in(key, 5), (rows, 1), jnp.float32, jnp.log(0.5), jnp.log(1.5)))
    col_scale = jax.random.uniform(jax.random.fold_in(key, 6), (1, cols), jnp.float32, 1.0, 1.0)
    return (noise * row_scale * col_scale / jnp.sqrt(jnp.float32(cols))).astype(jnp.bfloat16)


def noisy(key, rows, cols, limit):
    values = jax.random.normal(key, (rows, cols), jnp.float32)
    return jnp.clip(values, -limit, limit)


def draw_grad_q_up(key, part):
    key = jax.random.fold_in(key, 12)
    return scaled(key, noisy(key, M_QB, N_QB, 5.0))


def draw_grad_kv_down(key, part):
    key = jax.random.fold_in(key, 13)
    return scaled(key, noisy(key, M_KA, N_KA, 5.0))


def draw_grad_kv_up(key, part):
    key = jax.random.fold_in(key, 14)
    return scaled(key, noisy(key, M_KB, N_KB, 5.0))


def setup_inputs(seed: int = 0) -> dict:
    key_list = jax.random.split(jax.random.key(seed), 4)
    return {
        "grad_q_up": draw_grad_q_up(jax.random.fold_in(key_list[3], 71), 0),
        "grad_kv_down": draw_grad_kv_down(jax.random.fold_in(key_list[3], 71), 0),
        "grad_kv_up": draw_grad_kv_up(jax.random.fold_in(key_list[3], 71), 0),
    }


coef_a = 3.4445
coef_b = -4.775
coef_c = 2.0315

def newton_step(iterate):
    gram = lax.dot_general(iterate, iterate, (((1,), (1,)), ((), ())), preferred_element_type=jnp.float32)
    gram_b = gram.astype(jnp.bfloat16)
    first = jnp.dot(gram_b, iterate, preferred_element_type=jnp.float32)
    second = jnp.dot(gram_b, first.astype(jnp.bfloat16), preferred_element_type=jnp.float32)
    factor = math.sqrt(iterate.shape[1])
    mixed = coef_a * iterate.astype(jnp.float32) + coef_b * first + coef_c * second
    return (factor * mixed).astype(jnp.bfloat16)

def reference(grad_q_up, grad_kv_down, grad_kv_up):
    return (newton_step(grad_q_up), newton_step(grad_kv_down), newton_step(grad_kv_up))
```

```python
import functools
import math

import jax
import jax.numpy as jnp
from jax import lax
from jax.experimental import pallas as pl
from jax.experimental.pallas import tpu as pltpu
from jax.sharding import Mesh, PartitionSpec as P

coef_a = 3.4445
coef_b = -4.775
coef_c = 2.0315

bf16 = jnp.bfloat16
f32 = jnp.float32

QR, QC = 384, 384
DR, DC = 144, 112
UR, UC = 128, 512
NX, NY, NZ = 4, 4, 8
Q0, U0, D0 = 0, 1152, 1664
XROWS = 1808
GQ, GU, GD = 0, 4608, 5120
GEND = 5840
GROWS = 6144
HALF = GROWS // 2
PIECE = HALF // NY
SHARD = PIECE // NZ


def vmem(n):
    return [pl.BlockSpec(memory_space=pltpu.VMEM)] * n


def call(kernel, outs, scratch=(), flops=0):
    def run(*args):
        outs_t = tuple(jax.ShapeDtypeStruct(s, d) for s, d in outs)
        moved = sum(a.size * a.dtype.itemsize for a in args) + sum(
            s.size * s.dtype.itemsize for s in outs_t
        )
        return pl.pallas_call(
            kernel,
            out_shape=outs_t,
            in_specs=vmem(len(args)),
            out_specs=tuple(vmem(len(outs))),
            scratch_shapes=list(scratch),
            cost_estimate=pl.CostEstimate(flops=flops, bytes_accessed=moved, transcendentals=0),
            compiler_params=pltpu.CompilerParams(vmem_limit_bytes=40 << 20),
        )(*args)

    return run


def dot_t(a, b):
    return lax.dot_general(a, b, (((1,), (1,)), ((), ())), preferred_element_type=f32)


def dot(a, b):
    return jnp.dot(a, b, preferred_element_type=f32)


def q_of(p):
    return jnp.concatenate([p[Q0 + QR * k : Q0 + QR * (k + 1), :] for k in range(QC // 128)], axis=1)


def u_of(p):
    return jnp.concatenate([p[U0 + UR * k : U0 + UR * (k + 1), :] for k in range(UC // 128)], axis=1)


def d_of(p):
    return p[D0 : D0 + DR, :]


def pack_kernel(q, d, u, o):
    for k in range(QC // 128):
        o[Q0 + QR * k : Q0 + QR * (k + 1), :] = q[:, 128 * k : 128 * (k + 1)]
    for k in range(UC // 128):
        o[U0 + UR * k : U0 + UR * (k + 1), :] = u[:, 128 * k : 128 * (k + 1)]
    o[D0 : D0 + DR, :] = jnp.zeros((DR, 128), bf16)
    o[D0 : D0 + DR, 0:DC] = d[...]


def gram_kernel(p0, p1, p2, p3, keep, send):
    core = lax.axis_index("c")

    def put(low, high, row, value):
        ref = low if row < HALF else high
        at = row % HALF
        ref[at : at + value.shape[0], :] = value.astype(bf16)

    def emit(low, high):
        own = q_of(p0)
        for i, p in enumerate((p0, p1, p2, p3)):
            g = dot_t(own, q_of(p))
            for k in range(3):
                put(low, high, GQ + (3 * i + k) * QR, g[:, 128 * k : 128 * (k + 1)])
        own = u_of(p0)
        for i, p in enumerate((p0, p1, p2, p3)):
            put(low, high, GU + i * UR, dot_t(own, u_of(p)))
        everyone = jnp.concatenate([d_of(p) for p in (p0, p1, p2, p3)], axis=0)
        g = dot_t(d_of(p0), everyone)
        for k in range(4):
            put(low, high, GD + k * DR, g[:, 128 * k : 128 * (k + 1)])
        high[GD + 4 * DR - HALF : GROWS - HALF, :] = jnp.zeros((GROWS - GD - 4 * DR, 128), bf16)
        high[GD + 4 * DR - HALF : GEND - HALF, 0:64] = g[:, 512:576].astype(bf16)

    @pl.when(core == 0)
    def _():
        emit(keep, send)

    @pl.when(core == 1)
    def _():
        emit(send, keep)


def core_sum_kernel(keep, got, *outs):
    y = lax.axis_index("y")
    for i, o in enumerate(outs):
        at = pl.multiple_of(lax.rem(y + i, NY) * PIECE, PIECE)
        rows = pl.ds(at, PIECE)
        o[...] = (keep[rows, :].astype(f32) + got[rows, :].astype(f32)).astype(bf16)


def y_sum_kernel(a, b, c, d, o):
    o[...] = (
        (a[...].astype(f32) + b[...].astype(f32)) + (c[...].astype(f32) + d[...].astype(f32))
    ).astype(bf16)


def z_sum_kernel(a, o):
    total = a[0:SHARD, :].astype(f32)
    for i in range(1, NZ):
        total = total + a[SHARD * i : SHARD * (i + 1), :].astype(f32)
    total = total.astype(bf16)
    for i in range(NZ):
        o[SHARD * i : SHARD * (i + 1), :] = total


def products(gram, blocks):
    acc = None
    for i, p in enumerate(blocks):
        lhs = jnp.concatenate(
            [gram[GQ + (3 * i + k) * QR : GQ + (3 * i + k + 1) * QR, :] for k in range(3)], axis=1
        )
        term = dot(lhs, q_of(p))
        acc = term if acc is None else acc + term
    out_q = acc
    acc = None
    for i, p in enumerate(blocks):
        term = dot(gram[GU + i * UR : GU + (i + 1) * UR, :], u_of(p))
        acc = term if acc is None else acc + term
    out_u = acc
    lhs = jnp.concatenate(
        [gram[GD + k * DR : GD + (k + 1) * DR, :] for k in range(4)]
        + [gram[GD + 4 * DR : GD + 5 * DR, 0:64]],
        axis=1,
    )
    out_d = dot(lhs, jnp.concatenate([d_of(p) for p in blocks], axis=0))
    return out_q, out_d, out_u


def first_kernel(*refs):
    mine, other = refs[0:4], refs[4:8]
    blocks = refs[8:12]
    gram, first_b, acc = refs[12:15]
    y, core = lax.axis_index("y"), lax.axis_index("c")
    for group, which in ((mine, core), (other, 1 - core)):
        for i, piece in enumerate(group):
            at = which * HALF + lax.rem(y + NY - i, NY) * PIECE
            gram[pl.ds(pl.multiple_of(at, PIECE), PIECE), :] = piece[...]
    out_q, out_d, out_u = products(gram, blocks)

    def put(row, value):
        rows = slice(row, row + value.shape[0])
        first_b[rows, :] = value.astype(bf16)
        acc[rows, :] = coef_a * blocks[0][rows, :].astype(f32) + coef_b * value

    for k in range(QC // 128):
        put(Q0 + QR * k, out_q[:, 128 * k : 128 * (k + 1)])
    for k in range(UC // 128):
        put(U0 + UR * k, out_u[:, 128 * k : 128 * (k + 1)])
    put(D0, out_d)


def second_kernel(factors, gram, acc, f0, f1, f2, f3, step_q, step_d, step_u):
    out_q, out_d, out_u = products(gram, (f0, f1, f2, f3))
    fq, fd, fu = factors
    for k in range(QC // 128):
        lanes = slice(128 * k, 128 * (k + 1))
        step_q[:, lanes] = (
            fq * (acc[Q0 + QR * k : Q0 + QR * (k + 1), :] + coef_c * out_q[:, lanes])
        ).astype(bf16)
    for k in range(UC // 128):
        lanes = slice(128 * k, 128 * (k + 1))
        step_u[:, lanes] = (
            fu * (acc[U0 + UR * k : U0 + UR * (k + 1), :] + coef_c * out_u[:, lanes])
        ).astype(bf16)
    whole = (fd * (acc[D0 : D0 + DR, :] + coef_c * out_d)).astype(bf16)
    step_d[...] = whole[:, 0:DC]


def shift(value, axis, size, by):
    return lax.ppermute(value, axis, [(i, (i + by) % size) for i in range(size)])


def from_others(value, axis, size):
    return [value] + [shift(value, axis, size, i) for i in range(1, size)]


def shards(grad_q_up, grad_kv_down, grad_kv_up):
    columns = 64
    factors = tuple(math.sqrt(g.shape[1] * columns) for g in (grad_q_up, grad_kv_down, grad_kv_up))
    flops = 2 * 4 * (QR * QR * QC + UR * UR * UC + DR * DR * 128)
    (packed,) = call(pack_kernel, [((XROWS, 128), bf16)])(grad_q_up, grad_kv_down, grad_kv_up)
    blocks = from_others(packed, "x", NX)
    half = ((HALF, 128), bf16)
    piece = ((PIECE, 128), bf16)
    keep, send = call(gram_kernel, [half, half], flops=flops)(*blocks)
    got = shift(send, "c", 2, 1)
    pieces = call(core_sum_kernel, [piece] * NY)(keep, got)
    pieces = [pieces[0]] + [shift(pieces[i], "y", NY, i) for i in range(1, NY)]
    (total,) = call(y_sum_kernel, [piece])(*pieces)
    total = lax.all_to_all(total, "z", 0, 0, tiled=True)
    (total,) = call(z_sum_kernel, [piece])(total)
    total = lax.all_to_all(total, "z", 0, 0, tiled=True)
    mine = from_others(total, "y", NY)
    other = [shift(m, "c", 2, 1) for m in mine]
    gram, first_b, acc = call(
        first_kernel,
        [((GROWS, 128), bf16), ((XROWS, 128), bf16), ((XROWS, 128), f32)],
        flops=flops,
    )(*mine, *other, *blocks)
    firsts = from_others(first_b, "x", NX)
    return tuple(
        call(
            functools.partial(second_kernel, factors),
            [((QR, QC), bf16), ((DR, DC), bf16), ((UR, UC), bf16)],
            flops=flops,
        )(gram, acc, *firsts)
    )


def solution(mesh):
    fine = Mesh(mesh.devices.reshape(NY, NZ, 2, NX), ("y", "z", "c", "x"))
    placed = P("x", ("y", "z", "c"))
    return jax.shard_map(
        shards,
        mesh=fine,
        in_specs=(placed, placed, placed),
        out_specs=(placed, placed, placed),
        check_vma=False,
    )
```

```python
import functools
import math

import jax
import jax.numpy as jnp
from jax import lax
from jax.experimental import pallas as pl
from jax.experimental.pallas import tpu as pltpu
from jax.sharding import Mesh, PartitionSpec as P

coef_a = 3.4445
coef_b = -4.775
coef_c = 2.0315

bf16 = jnp.bfloat16
f32 = jnp.float32

QR, QC = 384, 384
DR, DC = 144, 112
UR, UC = 128, 512
QH = QR // 2
NX, NY, NZ = 4, 4, 8
NP = 2 * NY

X1 = 2 * QR + DR
XROWS = X1 + QR + UR * (UC // 128)
F1 = 3 * QH + 4 * UR
FCUT = 3 * QH + 3 * UR

A1, A2, B1, B2 = 272, 288, 96, 112
PA, PB = A1 + A2, B1 + B2
G1, G2 = A1 + B1, A2 + B2
PIECE = PA + PB
SHARD = PIECE // NZ
A_AT = 0
B1_AT, B2_AT = A1 * NP, A2 * NP


def vmem(n):
    return [pl.BlockSpec(memory_space=pltpu.VMEM)] * n


def call(kernel, outs, flops=0, scratch=(), hbm=(), after=(), limit=40):
    def run(*args):
        n = len(args)
        args = (*args, *after)
        outs_t = tuple(jax.ShapeDtypeStruct(s, d) for s, d in outs)
        moved = sum(a.size * a.dtype.itemsize for a in args) + sum(
            s.size * s.dtype.itemsize for s in outs_t
        )
        return pl.pallas_call(
            skip(kernel, n, len(after)),
            out_shape=outs_t,
            in_specs=[
                pl.BlockSpec(memory_space=pl.ANY if i in hbm or i >= n else pltpu.VMEM)
                for i in range(len(args))
            ],
            out_specs=tuple(vmem(len(outs))),
            scratch_shapes=list(scratch),
            cost_estimate=pl.CostEstimate(flops=flops, bytes_accessed=moved, transcendentals=0),
            compiler_params=pltpu.CompilerParams(vmem_limit_bytes=limit << 20),
        )(*args)

    return run


def skip(kernel, n, extra):
    return lambda *refs: kernel(*refs[:n], *refs[n + extra :])


def dot_t(a, b):
    return lax.dot_general(a, b, (((1,), (1,)), ((), ())), preferred_element_type=f32)


def dot(a, b):
    return jnp.dot(a, b, preferred_element_type=f32)


def lanes(parts):
    return jnp.concatenate(parts, axis=1)


def rows(parts):
    return jnp.concatenate(parts, axis=0)


def rows_of(block, lo, n):
    cut, parts = block
    if lo < cut:
        return parts[0][lo : lo + n, :]
    return parts[1][lo - cut : lo - cut + n, :]


def x_q(p):
    return lanes([rows_of(p, at, QR) for at in (0, QR, X1)])


def x_d(p):
    return rows_of(p, 2 * QR, DR)


def x_u(p):
    return lanes([rows_of(p, X1 + QR + UR * k, UR) for k in range(4)])


def f_q(p):
    return rows([lanes([rows_of(p, at + QH * k, QH) for k in range(3)]) for at in (0, F1)])


def f_d(p):
    return rows_of(p, F1 + 3 * QH, DR)


def f_u(p):
    return lanes([rows_of(p, 3 * QH + UR * k, UR) for k in range(4)])


def blocks_of(refs, cut):
    out = [(XROWS, (r,)) for r in refs[0:3]]
    return out + ([(cut, tuple(refs[3:5]))] if len(refs) == 5 else [])


def padded(parts, to):
    return rows(parts + [jnp.zeros((to - sum(p.shape[0] for p in parts), 128), bf16)])


def pack_kernel(q, d, u, o, held, sems):
    moves = [(d, held)]
    for k in range(2):
        moves.append((q.at[:, 128 * k : 128 * (k + 1)], o.at[QR * k : QR * (k + 1), :]))
    moves.append((q.at[:, 256:384], o.at[X1 : X1 + QR, :]))
    for k in range(4):
        at = slice(X1 + QR + UR * k, X1 + QR + UR * (k + 1))
        moves.append((u.at[:, 128 * k : 128 * (k + 1)], o.at[at, :]))
    copies = [pltpu.make_async_copy(a, b, sems.at[i]) for i, (a, b) in enumerate(moves)]
    for copy in copies:
        copy.start()
    copies[0].wait()
    o[2 * QR : X1, :] = jnp.zeros((DR, 128), bf16)
    o[2 * QR : X1, 0:DC] = held[...]
    for copy in copies[1:]:
        copy.wait()


def gram_kernel(*refs):
    every = blocks_of(refs[0:5], X1)
    own = every[0]
    keep, send = refs[5:7]
    core = lax.axis_index("c")

    def emit(low, high):
        def put(size, base, at, value):
            value = value.astype(bf16)
            done, n = 0, value.shape[0]
            while done < n:
                piece, off = divmod(at + done, size)
                m = min(n - done, size - off)
                ref = low if piece < NY else high
                to = (piece % NY) * PIECE + base + off
                ref[to : to + m, :] = value[done : done + m, :]
                done += m

        for blocks, upper, lower, base1, base2 in (
            (every[0:3], A1, A2, 0, G1),
            (every[3:4], B1, B2, A1, G1 + A2),
        ):
            count = len(blocks)
            mine = x_q(own)
            for i, p in enumerate(blocks):
                g = dot_t(mine, x_q(p))
                for k in range(3):
                    at = (3 * i + k) * QH
                    put(upper, base1, at, g[0:QH, 128 * k : 128 * (k + 1)])
                    put(lower, base2, at, g[QH:QR, 128 * k : 128 * (k + 1)])
            at = 3 * count * QH
            mine = x_u(own)
            for i, p in enumerate(blocks):
                put(upper, base1, at + UR * i, dot_t(mine, x_u(p)))
            end = at + UR * count
            if upper * NP > end:
                put(upper, base1, end, jnp.zeros((upper * NP - end, 128), f32))
            g = dot_t(x_d(own), padded([x_d(p) for p in blocks], 128 * (count + 1)))
            for k in range(count + 1):
                put(lower, base2, at + DR * k, g[:, 128 * k : 128 * (k + 1)])
            end = at + DR * (count + 1)
            if lower * NP > end:
                put(lower, base2, end, jnp.zeros((lower * NP - end, 128), f32))

    @pl.when(core == 0)
    def _():
        emit(keep, send)

    @pl.when(core == 1)
    def _():
        emit(send, keep)


def core_sum_kernel(keep, got, *outs):
    y = lax.axis_index("y")
    n = outs[0].shape[0]
    for i, o in enumerate(outs):
        at = pl.ds(pl.multiple_of(lax.rem(y + i, NY) * n, 16), n)
        o[...] = (keep[at, :].astype(f32) + got[at, :].astype(f32)).astype(bf16)


def y_sum_kernel(a, b, c, d, o):
    o[...] = (
        (a[...].astype(f32) + b[...].astype(f32)) + (c[...].astype(f32) + d[...].astype(f32))
    ).astype(bf16)


def z_sum_kernel(a, o):
    total = a[0:SHARD, :].astype(f32)
    for i in range(1, NZ):
        total = total + a[SHARD * i : SHARD * (i + 1), :].astype(f32)
    total = total.astype(bf16)
    for i in range(NZ):
        o[SHARD * i : SHARD * (i + 1), :] = total


def q_product(gram, b_at, q):
    out = None
    for i in range(4):
        base = b_at if i == 3 else 3 * i * QH
        lhs = lanes([gram[base + QH * k : base + QH * (k + 1), :] for k in range(3)])
        term = dot(lhs, q[i])
        out = term if out is None else out + term
    return out


def u_product(gram, blocks, u_of):
    out = None
    for i, p in enumerate(blocks):
        at = (B1_AT + 3 * QH) if i == 3 else 9 * QH + UR * i
        term = dot(gram[at : at + UR, :], u_of(p))
        out = term if out is None else out + term
    return out


def d_product(gram, blocks, d_of):
    lhs_a = lanes([gram[9 * QH + DR * k : 9 * QH + DR * (k + 1), :] for k in range(4)])
    at = B2_AT + 3 * QH
    lhs_b = lanes([gram[at + DR * k : at + DR * (k + 1), :] for k in range(2)])
    rhs_a = padded([d_of(p) for p in blocks[0:3]], 512)
    return dot(lhs_a, rhs_a) + dot(lhs_b, padded([d_of(blocks[3])], 256))


def unpack_gram(gram1, gram2, mine, other):
    y, core = lax.axis_index("y"), lax.axis_index("c")
    for group, which in ((mine, core), (other, 1 - core)):
        for i, piece in enumerate(group):
            p = which * NY + lax.rem(y + NY - i, NY)
            for gram, base, size, at in (
                (gram1, 0, A1, 0),
                (gram1, B1_AT, B1, A1),
                (gram2, 0, A2, G1),
                (gram2, B2_AT, B2, G1 + A2),
            ):
                to = pl.multiple_of(base + p * size, 16)
                gram[pl.ds(to, size), :] = piece[at : at + size, :]


def first_kernel(*refs):
    blocks = blocks_of(refs[8:13], X1)
    gram1, gram2, first_b, acc = refs[13:17]
    unpack_gram(gram1, gram2, refs[0:4], refs[4:8])

    def put(at, x, value):
        to = slice(at, at + value.shape[0])
        first_b[to, :] = value.astype(bf16)
        acc[to, :] = coef_a * x.astype(f32) + coef_b * value

    q = [x_q(p) for p in blocks]
    for h, (gram, b_at, base) in enumerate(((gram1, B1_AT, 0), (gram2, B2_AT, F1))):
        out = q_product(gram, b_at, q)
        for k in range(3):
            at = slice(128 * k, 128 * (k + 1))
            put(base + QH * k, q[0][QH * h : QH * (h + 1), at], out[:, at])
    out = u_product(gram1, blocks, x_u)
    x = x_u(blocks[0])
    for k in range(4):
        at = slice(128 * k, 128 * (k + 1))
        put(3 * QH + UR * k, x[:, at], out[:, at])
    put(F1 + 3 * QH, x_d(blocks[0]), d_product(gram2, blocks, x_d))


def second_kernel(factors, gram1, gram2, acc, *refs):
    blocks = blocks_of(refs[0:5], FCUT)
    step_q, step_d, step_u = refs[5:8]
    fq, fd, fu = factors
    q = [f_q(p) for p in blocks]
    for h, (gram, b_at, base) in enumerate(((gram1, B1_AT, 0), (gram2, B2_AT, F1))):
        out = q_product(gram, b_at, q)
        for k in range(3):
            at = slice(128 * k, 128 * (k + 1))
            rest = acc[base + QH * k : base + QH * (k + 1), :]
            step_q[QH * h : QH * (h + 1), at] = (fq * (rest + coef_c * out[:, at])).astype(bf16)
    out = u_product(gram1, blocks, f_u)
    for k in range(4):
        at = slice(128 * k, 128 * (k + 1))
        base = 3 * QH + UR * k
        step_u[:, at] = (fu * (acc[base : base + UR, :] + coef_c * out[:, at])).astype(bf16)
    out = d_product(gram2, blocks, f_d)
    base = F1 + 3 * QH
    step_d[...] = (fd * (acc[base : base + DR, :] + coef_c * out)).astype(bf16)[:, 0:DC]


def shift(value, axis, size, by):
    return lax.ppermute(value, axis, [(i, (i + by) % size) for i in range(size)])


def ring(own, cut):
    left, right = shift(own, "x", NX, 1), shift(own, "x", NX, -1)
    return [own, left, right, shift(left[0:cut], "x", NX, 1), shift(right[cut:], "x", NX, -1)]


def sum_y(keep, send, n):
    got = shift(send, "c", 2, 1)
    pieces = call(core_sum_kernel, [((n, 128), bf16)] * NY)(keep, got)
    return [pieces[0]] + [shift(pieces[i], "y", NY, i) for i in range(1, NY)]


def gather_y(part):
    mine = [part] + [shift(part, "y", NY, i) for i in range(1, NY)]
    return mine + [shift(m, "c", 2, 1) for m in mine]


def shards(grad_q_up, grad_kv_down, grad_kv_up):
    columns = NP * NZ
    factors = tuple(math.sqrt(g.shape[1] * columns) for g in (grad_q_up, grad_kv_down, grad_kv_up))
    flops = 2 * 4 * (QR * QR * QC + UR * UR * UC + DR * DR * 128)
    (packed,) = call(
        pack_kernel,
        [((XROWS, 128), bf16)],
        scratch=[pltpu.VMEM((DR, DC), bf16), pltpu.SemaphoreType.DMA((8,))],
        hbm=(0, 1, 2),
        limit=60,
    )(grad_q_up, grad_kv_down, grad_kv_up)
    x = ring(packed, X1)
    keep, send = call(gram_kernel, [((NY * PIECE, 128), bf16)] * 2, flops)(*x)
    (total,) = call(y_sum_kernel, [((PIECE, 128), bf16)])(*sum_y(keep, send, PIECE))
    total = lax.all_to_all(total, "z", 0, 0, tiled=True)
    (total,) = call(z_sum_kernel, [((PIECE, 128), bf16)])(total)
    total = lax.all_to_all(total, "z", 0, 0, tiled=True)
    gram1, gram2, first_b, acc = call(
        first_kernel,
        [
            ((NP * G1, 128), bf16),
            ((NP * G2, 128), bf16),
            ((XROWS, 128), bf16),
            ((XROWS, 128), f32),
        ],
        flops,
    )(*gather_y(total), *x)
    return tuple(
        call(
            functools.partial(second_kernel, factors),
            [((QR, QC), bf16), ((DR, DC), bf16), ((UR, UC), bf16)],
            flops,
        )(gram1, gram2, acc, *ring(first_b, FCUT))
    )


def solution(mesh):
    fine = Mesh(mesh.devices.reshape(NY, NZ, 2, NX), ("y", "z", "c", "x"))
    placed = P("x", ("y", "z", "c"))
    return jax.shard_map(
        shards,
        mesh=fine,
        in_specs=(placed, placed, placed),
        out_specs=(placed, placed, placed),
        check_vma=False,
    )
```

```python
import functools
import math

import jax
import jax.numpy as jnp
from jax import lax
from jax.experimental import pallas as pl
from jax.experimental.pallas import tpu as pltpu
from jax.sharding import Mesh, PartitionSpec as P

coef_a = 3.4445
coef_b = -4.775
coef_c = 2.0315

bf16 = jnp.bfloat16
f32 = jnp.float32

QR, QC = 384, 384
DR, DC = 144, 112
UR, UC = 128, 512
NX, NY, NZ = 4, 4, 8
NP = 2 * NY

X1 = 2 * QR + DR
XROWS = X1 + QR + UR * (UC // 128)

QH, UH, DU = QR // 2, UR // 2, 80
DL = DR - DU

D, P_, C, S = 0, 192, 288, 384
PG = 480
SHARD = 64
SENT = SHARD * NZ
HELD = (("D", 192), ("P", 96), ("S", 96), ("LP", 96), ("LC", 96), ("RC", 96), ("RS", 96))
PIECE = 768
BASE = {"D": 0, "P": 1536, "S": 2304, "LP": 3072, "LC": 3840, "RC": 4608, "RS": 5376}
GROWS = 6144


def vmem(n):
    return [pl.BlockSpec(memory_space=pltpu.VMEM)] * n


def call(kernel, outs, flops=0, scratch=(), hbm=(), after=(), limit=40):
    def run(*args):
        n = len(args)
        args = (*args, *after)
        outs_t = tuple(jax.ShapeDtypeStruct(s, d) for s, d in outs)
        moved = sum(a.size * a.dtype.itemsize for a in args) + sum(
            s.size * s.dtype.itemsize for s in outs_t
        )
        return pl.pallas_call(
            skip(kernel, n, len(after)),
            out_shape=outs_t,
            in_specs=[
                pl.BlockSpec(memory_space=pl.ANY if i in hbm or i >= n else pltpu.VMEM)
                for i in range(len(args))
            ],
            out_specs=tuple(vmem(len(outs))),
            scratch_shapes=list(scratch),
            cost_estimate=pl.CostEstimate(flops=flops, bytes_accessed=moved, transcendentals=0),
            compiler_params=pltpu.CompilerParams(vmem_limit_bytes=limit << 20),
        )(*args)

    return run


def skip(kernel, n, extra):
    return lambda *refs: kernel(*refs[:n], *refs[n + extra :])


def dot_t(a, b):
    return lax.dot_general(a, b, (((1,), (1,)), ((), ())), preferred_element_type=f32)


def dot(a, b):
    return jnp.dot(a, b, preferred_element_type=f32)


def lanes(parts):
    return jnp.concatenate(parts, axis=1)


def rows(parts):
    return jnp.concatenate(parts, axis=0)


def rows_of(block, lo, n):
    cut, parts = block
    if lo < cut:
        return parts[0][lo : lo + n, :]
    return parts[1][lo - cut : lo - cut + n, :]


def x_q(p):
    return lanes([rows_of(p, at, QR) for at in (0, QR, X1)])


def x_d(p):
    return rows_of(p, 2 * QR, DR)


def x_u(p):
    return lanes([rows_of(p, X1 + QR + UR * k, UR) for k in range(4)])


def dot_l(a, b):
    return lax.dot_general(a, b, (((0,), (0,)), ((), ())), preferred_element_type=f32)


def blocks_of(refs, cut):
    out = [(XROWS, (r,)) for r in refs[0:3]]
    return out + ([(cut, tuple(refs[3:5]))] if len(refs) == 5 else [])


def padded(v, to):
    return rows([v, jnp.zeros((to - v.shape[0], v.shape[1]), v.dtype)])


def pack_kernel(q, d, u, o, held, sems):
    moves = [(d, held)]
    for k in range(2):
        moves.append((q.at[:, 128 * k : 128 * (k + 1)], o.at[QR * k : QR * (k + 1), :]))
    moves.append((q.at[:, 256:384], o.at[X1 : X1 + QR, :]))
    for k in range(4):
        at = slice(X1 + QR + UR * k, X1 + QR + UR * (k + 1))
        moves.append((u.at[:, 128 * k : 128 * (k + 1)], o.at[at, :]))
    copies = [pltpu.make_async_copy(a, b, sems.at[i]) for i, (a, b) in enumerate(moves)]
    for copy in copies:
        copy.start()
    copies[0].wait()
    o[2 * QR : X1, :] = jnp.zeros((DR, 128), bf16)
    o[2 * QR : X1, 0:DC] = held[...]
    for copy in copies[1:]:
        copy.wait()


def half_products(a, b, upper):
    g = dot_t(x_q(a)[0:QH] if upper else x_q(a)[QH:QR], x_q(b))
    out = [(QH * k, g[:, 128 * k : 128 * (k + 1)]) for k in range(3)]
    at = 3 * QH
    out.append((at, dot_t(x_u(a)[0:UH] if upper else x_u(a)[UH:UR], x_u(b))))
    at += UH
    mine = x_d(a)[0:DU] if upper else x_d(a)[DU:DR]
    out.append((at, dot_t(mine, x_d(b)[0:128])))
    at += mine.shape[0]
    out.append((at, dot_t(x_d(b)[128:DR], padded(mine, 128))))
    at += DR - 128
    out.append((at, jnp.zeros((96 * NP - at, 128), f32)))
    return out


def gram_kernel(*refs):
    own, left, right = blocks_of(refs[0:3], 0)
    keep, send = refs[3:5]

    def put(low, high, size, base, at, value):
        value = value.astype(bf16)
        done, n = 0, value.shape[0]
        while done < n:
            piece, off = divmod(at + done, size)
            m = min(n - done, size - off)
            ref = low if piece < NY else high
            to = (piece % NY) * PG + base + off
            ref[to : to + m, :] = value[done : done + m, :]
            done += m

    def emit(low, high):
        g = dot_t(x_q(own), x_q(own))
        for k in range(3):
            put(low, high, 192, D, QR * k, g[:, 128 * k : 128 * (k + 1)])
        put(low, high, 192, D, 3 * QR, dot_t(x_u(own), x_u(own)))
        g = dot_t(x_d(own), padded(x_d(own), 256))
        at = 3 * QR + UR
        put(low, high, 192, D, at, g[:, 0:128])
        put(low, high, 192, D, at + DR, g[128:DR, 128:256])
        at += DR + DR - 128
        put(low, high, 192, D, at, jnp.zeros((192 * NP - at, 128), f32))
        for at, value in half_products(own, right, True):
            put(low, high, 96, P_, at, value)
        for at, value in half_products(left, own, False):
            put(low, high, 96, S, at, value)

    def emit_cross(low, high, a, b, upper):
        for at, value in half_products(a, b, upper):
            put(low, high, 96, C, at, value)

    core = lax.axis_index("c")
    first_two = lax.axis_index("x") < 2
    for mine, low, high in ((0, keep, send), (1, send, keep)):

        @pl.when(core == mine)
        def _():
            emit(low, high)

        @pl.when(jnp.logical_and(core == mine, first_two))
        def _():
            emit_cross(low, high, left, right, True)

        @pl.when(jnp.logical_and(core == mine, jnp.logical_not(first_two)))
        def _():
            emit_cross(low, high, right, left, False)


def core_sum_kernel(keep, got, *outs):
    y = lax.axis_index("y")
    n = outs[0].shape[0]
    for i, o in enumerate(outs):
        at = pl.ds(pl.multiple_of(lax.rem(y + i, NY) * n, 16), n)
        o[...] = (keep[at, :].astype(f32) + got[at, :].astype(f32)).astype(bf16)


def y_sum_kernel(a, b, c, d, o):
    o[0:PG, :] = (
        (a[...].astype(f32) + b[...].astype(f32)) + (c[...].astype(f32) + d[...].astype(f32))
    ).astype(bf16)
    o[PG:SENT, :] = jnp.zeros((SENT - PG, 128), bf16)


def z_sum_kernel(a, o):
    total = a[0:SHARD, :].astype(f32)
    for i in range(1, NZ):
        total = total + a[SHARD * i : SHARD * (i + 1), :].astype(f32)
    total = total.astype(bf16)
    for i in range(NZ):
        o[SHARD * i : SHARD * (i + 1), :] = total


def join_kernel(own, left, right, o):
    o[0:288, :] = own[0:288, :]
    o[288:384, :] = own[S : S + 96, :]
    o[384:576, :] = left[...]
    o[576:768, :] = right[...]


def unpack_gram(gram, mine, other):
    y, core = lax.axis_index("y"), lax.axis_index("c")
    for group, which in ((mine, core), (other, 1 - core)):
        for i, piece in enumerate(group):
            p = which * NY + lax.rem(y + NY - i, NY)
            at = 0
            for name, size in HELD:
                to = pl.multiple_of(BASE[name] + p * size, 16)
                gram[pl.ds(to, size), :] = piece[at : at + size, :]
                at += size


def half_q(gram, name):
    return lanes([gram[BASE[name] + QH * k : BASE[name] + QH * (k + 1), :] for k in range(3)])


def half_u(gram, name):
    at = BASE[name] + 3 * QH
    return gram[at : at + UH, :]


def half_d(gram, name, n):
    at = BASE[name] + 3 * QH + UH
    return gram[at : at + n, :], gram[at + n : at + n + DR - 128, :]


def straight(gram, upper, lower, b):
    q = dot(rows([half_q(gram, upper), half_q(gram, lower)]), x_q(b))
    u = dot(rows([half_u(gram, upper), half_u(gram, lower)]), x_u(b))
    main, rest = x_d(b)[0:128], x_d(b)[128:DR]
    parts = []
    for name, n in ((upper, DU), (lower, DL)):
        lead, last = half_d(gram, name, n)
        parts.append(dot(lead, main) + dot_l(last, rest)[0:n])
    return q, rows(parts), u


def turned(gram, upper, lower, b):
    q = dot_l(rows([half_q(gram, upper), half_q(gram, lower)]), x_q(b))
    u = dot_l(rows([half_u(gram, upper), half_u(gram, lower)]), x_u(b))
    d = None
    for name, n, v in ((upper, DU, x_d(b)[0:DU]), (lower, DL, x_d(b)[DU:DR])):
        lead, last = half_d(gram, name, n)
        term = rows([dot_l(lead, v), dot(last, padded(v, 128))])
        d = term if d is None else d + term
    return q, d, u


def own_product(gram, b):
    q = dot(lanes([gram[QR * k : QR * (k + 1), :] for k in range(3)]), x_q(b))
    at = 3 * QR
    u = dot(gram[at : at + UR, :], x_u(b))
    at += UR
    lead, last = gram[at : at + DR, :], gram[at + DR : at + DR + DR - 128, :]
    main, rest = x_d(b)[0:128], x_d(b)[128:DR]
    side = rows([dot_l(lead[128:DR], rest), dot(last, padded(rest, 128))])
    return q, dot(lead, main) + side, u


def added(*terms):
    out = terms[0]
    for t in terms[1:]:
        out = tuple(a + b for a, b in zip(out, t))
    return out


def near_product(gram, own, left, right):
    return added(
        own_product(gram, own),
        straight(gram, "P", "RS", right),
        turned(gram, "LP", "S", left),
    )


def far_product(gram, block, use):
    x = lax.axis_index("x")
    outer = jnp.logical_or(x == 0, x == 3)

    @pl.when(outer)
    def _():
        use(straight(gram, "RC", "LC", block))

    @pl.when(jnp.logical_not(outer))
    def _():
        use(turned(gram, "LC", "RC", block))


def packed_parts(value):
    q, d, u = value
    out = [(at, q[:, 128 * k : 128 * (k + 1)]) for k, at in enumerate((0, QR, X1))]
    out.append((2 * QR, d))
    return out + [(X1 + QR + UR * k, u[:, 128 * k : 128 * (k + 1)]) for k in range(4)]


def first_kernel(*refs):
    own, left, right, far = blocks_of(refs[8:13], X1)
    gram, first_b, acc = refs[13:16]
    unpack_gram(gram, refs[0:4], refs[4:8])
    near = near_product(gram, own, left, right)

    def use(value):
        for at, v in packed_parts(added(near, value)):
            to = slice(at, at + v.shape[0])
            first_b[to, :] = v.astype(bf16)
            acc[to, :] = coef_a * refs[8][to, :].astype(f32) + coef_b * v

    far_product(gram, far, use)


def second_near_kernel(gram, acc, own, left, right, total):
    for at, v in packed_parts(near_product(gram, *blocks_of((own, left, right), 0))):
        to = slice(at, at + v.shape[0])
        total[to, :] = acc[to, :] + coef_c * v


def second_far_kernel(factors, gram, total, o1, o2, step_q, step_d, step_u):
    fq, fd, fu = factors

    def use(value):
        parts = packed_parts(value)
        done = [total[at : at + v.shape[0], :] + coef_c * v for at, v in parts]
        for k in range(3):
            step_q[:, 128 * k : 128 * (k + 1)] = (fq * done[k]).astype(bf16)
        step_d[...] = (fd * done[3]).astype(bf16)[:, 0:DC]
        for k in range(4):
            step_u[:, 128 * k : 128 * (k + 1)] = (fu * done[4 + k]).astype(bf16)

    far_product(gram, (X1, (o1, o2)), use)


def shift(value, axis, size, by):
    return lax.ppermute(value, axis, [(i, (i + by) % size) for i in range(size)])


def ring(own):
    left, right = shift(own, "x", NX, 1), shift(own, "x", NX, -1)
    return [own, left, right, shift(left[0:X1], "x", NX, 1), shift(right[X1:], "x", NX, -1)]


def sum_y(keep, send):
    got = shift(send, "c", 2, 1)
    pieces = call(core_sum_kernel, [((PG, 128), bf16)] * NY)(keep, got)
    got = {i: shift(pieces[i], "y", NY, i) for i in (2, 1, 3)}
    return [pieces[0], got[1], got[2], got[3]]


def gather_y(part):
    got = {i: shift(part, "y", NY, i) for i in (2, 1, 3)}
    mine = [part, got[1], got[2], got[3]]
    return mine + [shift(m, "c", 2, 1) for m in mine]


def shards(grad_q_up, grad_kv_down, grad_kv_up):
    columns = NP * NZ
    factors = tuple(math.sqrt(g.shape[1] * columns) for g in (grad_q_up, grad_kv_down, grad_kv_up))
    flops = 2 * 4 * (QR * QR * QC + UR * UR * UC + DR * DR * 128)
    (packed,) = call(
        pack_kernel,
        [((XROWS, 128), bf16)],
        scratch=[pltpu.VMEM((DR, DC), bf16), pltpu.SemaphoreType.DMA((8,))],
        hbm=(0, 1, 2),
        limit=60,
    )(grad_q_up, grad_kv_down, grad_kv_up)
    x = ring(packed)
    keep, send = call(gram_kernel, [((NY * PG, 128), bf16)] * 2, flops)(*x[0:3])
    (total,) = call(y_sum_kernel, [((SENT, 128), bf16)])(*sum_y(keep, send))
    total = lax.all_to_all(total, "z", 0, 0, tiled=True)
    (total,) = call(z_sum_kernel, [((SENT, 128), bf16)])(total)
    total = lax.all_to_all(total, "z", 0, 0, tiled=True)
    left = shift(total[P_:S], "x", NX, 1)
    right = shift(total[C:PG], "x", NX, -1)
    (piece,) = call(join_kernel, [((PIECE, 128), bf16)])(total, left, right)
    gram, first_b, acc = call(
        first_kernel,
        [((GROWS, 128), bf16), ((XROWS, 128), bf16), ((XROWS, 128), f32)],
        flops,
    )(*gather_y(piece), *x)
    f = ring(first_b)
    (total,) = call(second_near_kernel, [((XROWS, 128), f32)], 3 * flops // 4)(gram, acc, *f[0:3])
    return tuple(
        call(
            functools.partial(second_far_kernel, factors),
            [((QR, QC), bf16), ((DR, DC), bf16), ((UR, UC), bf16)],
            flops // 4,
        )(gram, total, *f[3:5])
    )


def solution(mesh):
    fine = Mesh(mesh.devices.reshape(NY, NZ, 2, NX), ("y", "z", "c", "x"))
    placed = P("x", ("y", "z", "c"))
    return jax.shard_map(
        shards,
        mesh=fine,
        in_specs=(placed, placed, placed),
        out_specs=(placed, placed, placed),
        check_vma=False,
    )
```

```python
import functools
import math

import jax
import jax.numpy as jnp
from jax import lax
from jax.experimental import pallas as pl
from jax.experimental.pallas import tpu as pltpu
from jax.sharding import Mesh, PartitionSpec as P

coef_a = 3.4445
coef_b = -4.775
coef_c = 2.0315

bf16 = jnp.bfloat16
f32 = jnp.float32

QR, QC = 384, 384
DR, DC = 144, 112
UR, UC = 128, 512
NX, NY, NZ = 4, 4, 8
NP = 2 * NY

X1 = 2 * QR + DR
XROWS = X1 + QR + UR * (UC // 128)

QH, UH, DU = QR // 2, UR // 2, 80
DL = DR - DU

DN = 144
D, P_, C, S = 0, DN, DN + 96, DN + 192
PG = DN + 288
SHARD = 64
SENT = SHARD * NZ
HELD = (("D", DN), ("P", 96), ("S", 96), ("LP", 96), ("LC", 96), ("RC", 96), ("RS", 96))
PIECE = DN + 576
BASE = {name: NP * (DN * (i > 0) + 96 * max(i - 1, 0)) for i, (name, _) in enumerate(HELD)}
GROWS = NP * PIECE
DQ = (0, QR, 2 * QR - 128, 2 * QR)


def vmem(n):
    return [pl.BlockSpec(memory_space=pltpu.VMEM)] * n


def call(kernel, outs, flops=0, scratch=(), hbm=(), after=()):
    def run(*args):
        n = len(args)
        args = (*args, *after)
        outs_t = tuple(jax.ShapeDtypeStruct(s, d) for s, d in outs)
        moved = sum(a.size * a.dtype.itemsize for a in args) + sum(
            s.size * s.dtype.itemsize for s in outs_t
        )
        return pl.pallas_call(
            skip(kernel, n, len(after)),
            out_shape=outs_t,
            in_specs=[
                pl.BlockSpec(memory_space=pltpu.HBM if i in hbm else pl.ANY if i >= n else pltpu.VMEM)
                for i in range(len(args))
            ],
            out_specs=tuple(vmem(len(outs))),
            scratch_shapes=list(scratch),
            cost_estimate=pl.CostEstimate(flops=flops, bytes_accessed=moved, transcendentals=0),
            compiler_params=pltpu.CompilerParams(vmem_limit_bytes=40 << 20),
        )(*args)

    return run


def skip(kernel, n, extra):
    return lambda *refs: kernel(*refs[:n], *refs[n + extra :])


def dot_t(a, b):
    return lax.dot_general(a, b, (((1,), (1,)), ((), ())), preferred_element_type=f32)


def dot(a, b):
    return jnp.dot(a, b, preferred_element_type=f32)


def lanes(parts):
    return jnp.concatenate(parts, axis=1)


def rows(parts):
    return jnp.concatenate(parts, axis=0)


def rows_of(block, lo, n):
    cut, parts = block
    if lo < cut:
        return parts[0][lo : lo + n, :]
    return parts[1][lo - cut : lo - cut + n, :]


def x_q(p):
    return lanes([rows_of(p, at, QR) for at in (0, QR, X1)])


def x_d(p):
    return rows_of(p, 2 * QR, DR)


def x_u(p):
    return lanes([rows_of(p, X1 + QR + UR * k, UR) for k in range(4)])


def dot_l(a, b):
    return lax.dot_general(a, b, (((0,), (0,)), ((), ())), preferred_element_type=f32)


def blocks_of(refs, cut):
    out = [(XROWS, (r,)) for r in refs[0:3]]
    return out + ([(cut, tuple(refs[3:5]))] if len(refs) == 5 else [])


def padded(v, to):
    return rows([v, jnp.zeros((to - v.shape[0], v.shape[1]), v.dtype)])


def pack_kernel(q, d, u, o, held, sems):
    moves = [(d, held)]
    for k in range(2):
        moves.append((q.at[:, 128 * k : 128 * (k + 1)], o.at[QR * k : QR * (k + 1), :]))
    moves.append((q.at[:, 256:384], o.at[X1 : X1 + QR, :]))
    for k in range(4):
        at = slice(X1 + QR + UR * k, X1 + QR + UR * (k + 1))
        moves.append((u.at[:, 128 * k : 128 * (k + 1)], o.at[at, :]))
    copies = [pltpu.make_async_copy(a, b, sems.at[i]) for i, (a, b) in enumerate(moves)]
    for copy in copies:
        copy.start()
    copies[0].wait()
    o[2 * QR : X1, :] = jnp.zeros((DR, 128), bf16)
    o[2 * QR : X1, 0:DC] = held[...]
    for copy in copies[1:]:
        copy.wait()


def half_products(a, b, upper):
    g = dot_t(x_q(a)[0:QH] if upper else x_q(a)[QH:QR], x_q(b))
    out = [(QH * k, g[:, 128 * k : 128 * (k + 1)]) for k in range(3)]
    at = 3 * QH
    out.append((at, dot_t(x_u(a)[0:UH] if upper else x_u(a)[UH:UR], x_u(b))))
    at += UH
    mine = x_d(a)[0:DU] if upper else x_d(a)[DU:DR]
    out.append((at, dot_t(mine, x_d(b)[0:128])))
    at += mine.shape[0]
    out.append((at, dot_t(x_d(b)[128:DR], padded(mine, 128))))
    at += DR - 128
    out.append((at, jnp.zeros((96 * NP - at, 128), f32)))
    return out


def gram_kernel(near, *refs):
    own = (XROWS, (refs[0],))
    left, right = ((XROWS, (r,)) for r in refs[1:3]) if near else (None, None)
    keep, send = refs[-2:]
    total = PG - DN if near else DN

    def put(low, high, size, base, at, value):
        value = value.astype(bf16)
        done, n = 0, value.shape[0]
        while done < n:
            piece, off = divmod(at + done, size)
            m = min(n - done, size - off)
            ref = low if piece < NY else high
            to = (piece % NY) * total + base + off
            ref[to : to + m, :] = value[done : done + m, :]
            done += m

    def emit_own(low, high):
        g = dot_t(x_q(own), x_q(own))
        for k, at in enumerate(DQ):
            put(low, high, DN, D, at, g[128 * k : QR, 128 * k : 128 * (k + 1)])
        at = DQ[3]
        put(low, high, DN, D, at, dot_t(x_u(own), x_u(own)))
        g = dot_t(x_d(own), padded(x_d(own), 256))
        at += UR
        put(low, high, DN, D, at, g[:, 0:128])
        put(low, high, DN, D, at + DR, g[128:DR, 128:256])
        at += DR + DR - 128
        put(low, high, DN, D, at, jnp.zeros((DN * NP - at, 128), f32))

    def emit(low, high):
        if not near:
            emit_own(low, high)
            return
        for at, value in half_products(own, right, True):
            put(low, high, 96, P_ - DN, at, value)
        for at, value in half_products(left, own, False):
            put(low, high, 96, S - DN, at, value)

    def emit_cross(low, high, a, b, upper):
        for at, value in half_products(a, b, upper):
            put(low, high, 96, C - DN, at, value)

    core = lax.axis_index("c")
    first_two = lax.axis_index("x") < 2
    for mine, low, high in ((0, keep, send), (1, send, keep)):

        @pl.when(core == mine)
        def _():
            emit(low, high)

        if not near:
            continue

        @pl.when(jnp.logical_and(core == mine, first_two))
        def _():
            emit_cross(low, high, left, right, True)

        @pl.when(jnp.logical_and(core == mine, jnp.logical_not(first_two)))
        def _():
            emit_cross(low, high, right, left, False)


def core_sum_kernel(keep, got, *outs):
    y = lax.axis_index("y")
    n = outs[0].shape[0]
    for i, o in enumerate(outs):
        at = pl.ds(pl.multiple_of(lax.rem(y + i, NY) * n, 16), n)
        o[...] = (keep[at, :].astype(f32) + got[at, :].astype(f32)).astype(bf16)


def total_of(a, b, c, d):
    return (
        (a[...].astype(f32) + b[...].astype(f32)) + (c[...].astype(f32) + d[...].astype(f32))
    ).astype(bf16)


def own_sum_kernel(a, b, c, d, o):
    o[...] = total_of(a, b, c, d)


def y_sum_kernel(own, a, b, c, d, o):
    o[0:DN, :] = own[...]
    o[DN:PG, :] = total_of(a, b, c, d)
    o[PG:SENT, :] = jnp.zeros((SENT - PG, 128), bf16)


def z_sum_kernel(a, o):
    total = a[0:SHARD, :].astype(f32)
    for i in range(1, NZ):
        total = total + a[SHARD * i : SHARD * (i + 1), :].astype(f32)
    total = total.astype(bf16)
    for i in range(NZ):
        o[SHARD * i : SHARD * (i + 1), :] = total


def join_kernel(own, left, right, o):
    o[0:C, :] = own[0:C, :]
    o[C:S, :] = own[S:PG, :]
    o[S : S + 192, :] = left[...]
    o[S + 192 : PIECE, :] = right[...]


def unpack_gram(gram, mine, other):
    y, core = lax.axis_index("y"), lax.axis_index("c")
    for group, which in ((mine, core), (other, 1 - core)):
        for i, piece in enumerate(group):
            p = which * NY + lax.rem(y + NY - i, NY)
            at = 0
            for name, size in HELD:
                to = pl.multiple_of(BASE[name] + p * size, 16)
                gram[pl.ds(to, size), :] = piece[at : at + size, :]
                at += size


def half_q(gram, name):
    return lanes([gram[BASE[name] + QH * k : BASE[name] + QH * (k + 1), :] for k in range(3)])


def half_u(gram, name):
    at = BASE[name] + 3 * QH
    return gram[at : at + UH, :]


def half_d(gram, name, n):
    at = BASE[name] + 3 * QH + UH
    return gram[at : at + n, :], gram[at + n : at + n + DR - 128, :]


def straight(gram, upper, lower, b):
    q = dot(rows([half_q(gram, upper), half_q(gram, lower)]), x_q(b))
    u = dot(rows([half_u(gram, upper), half_u(gram, lower)]), x_u(b))
    main, rest = x_d(b)[0:128], x_d(b)[128:DR]
    parts = []
    for name, n in ((upper, DU), (lower, DL)):
        lead, last = half_d(gram, name, n)
        parts.append(dot(lead, main) + dot_l(last, rest)[0:n])
    return q, rows(parts), u


def turned(gram, upper, lower, b):
    q = dot_l(rows([half_q(gram, upper), half_q(gram, lower)]), x_q(b))
    u = dot_l(rows([half_u(gram, upper), half_u(gram, lower)]), x_u(b))
    d = None
    for name, n, v in ((upper, DU, x_d(b)[0:DU]), (lower, DL, x_d(b)[DU:DR])):
        lead, last = half_d(gram, name, n)
        term = rows([dot_l(lead, v), dot(last, padded(v, 128))])
        d = term if d is None else d + term
    return q, d, u


def own_product(gram, b):
    x = x_q(b)
    g0, g1, g2 = (gram[DQ[k] : DQ[k + 1], :] for k in range(3))
    q0, q1, q2 = (dot(g, x[128 * k : 128 * (k + 1)]) for k, g in enumerate((g0, g1, g2)))
    q = rows(
        [
            q0[0:128] + dot_l(g0[128:384], x[128:384]),
            q0[128:256] + q1[0:128] + dot_l(g1[128:256], x[256:384]),
            q0[256:384] + q1[128:256] + q2,
        ]
    )
    at = DQ[3]
    u = dot(gram[at : at + UR, :], x_u(b))
    at += UR
    lead, last = gram[at : at + DR, :], gram[at + DR : at + DR + DR - 128, :]
    main, rest = x_d(b)[0:128], x_d(b)[128:DR]
    side = rows([dot_l(lead[128:DR], rest), dot(last, padded(rest, 128))])
    return q, dot(lead, main) + side, u


def added(*terms):
    out = terms[0]
    for t in terms[1:]:
        out = tuple(a + b for a, b in zip(out, t))
    return out


def near_product(gram, own, left, right):
    return added(
        own_product(gram, own),
        straight(gram, "P", "RS", right),
        turned(gram, "LP", "S", left),
    )


def far_product(gram, block, use):
    x = lax.axis_index("x")
    outer = jnp.logical_or(x == 0, x == 3)

    @pl.when(outer)
    def _():
        use(straight(gram, "RC", "LC", block))

    @pl.when(jnp.logical_not(outer))
    def _():
        use(turned(gram, "LC", "RC", block))


def packed_parts(value):
    q, d, u = value
    out = [(at, q[:, 128 * k : 128 * (k + 1)]) for k, at in enumerate((0, QR, X1))]
    out.append((2 * QR, d))
    return out + [(X1 + QR + UR * k, u[:, 128 * k : 128 * (k + 1)]) for k in range(4)]


def first_kernel(*refs):
    own, left, right, far = blocks_of(refs[8:13], X1)
    gram, first_b, acc = refs[13:16]
    unpack_gram(gram, refs[0:4], refs[4:8])
    near = near_product(gram, own, left, right)

    def use(value):
        for at, v in packed_parts(added(near, value)):
            to = slice(at, at + v.shape[0])
            first_b[to, :] = v.astype(bf16)
            acc[to, :] = coef_a * refs[8][to, :].astype(f32) + coef_b * v

    far_product(gram, far, use)


def second_near_kernel(gram, acc, own, left, right, total):
    for at, v in packed_parts(near_product(gram, *blocks_of((own, left, right), 0))):
        to = slice(at, at + v.shape[0])
        total[to, :] = acc[to, :] + coef_c * v


def second_far_kernel(factors, gram, total, o1, o2, step_q, step_d, step_u):
    fq, fd, fu = factors

    def use(value):
        parts = packed_parts(value)
        done = [total[at : at + v.shape[0], :] + coef_c * v for at, v in parts]
        for k in range(3):
            step_q[:, 128 * k : 128 * (k + 1)] = (fq * done[k]).astype(bf16)
        step_d[...] = (fd * done[3]).astype(bf16)[:, 0:DC]
        for k in range(4):
            step_u[:, 128 * k : 128 * (k + 1)] = (fu * done[4 + k]).astype(bf16)

    far_product(gram, (X1, (o1, o2)), use)


def shift(value, axis, size, by):
    return lax.ppermute(value, axis, [(i, (i + by) % size) for i in range(size)])


def ring(own):
    left, right = shift(own, "x", NX, 1), shift(own, "x", NX, -1)
    return [own, left, right, shift(left[0:X1], "x", NX, 1), shift(right[X1:], "x", NX, -1)]


def sum_y(keep, send, n):
    got = shift(send, "c", 2, 1)
    pieces = call(core_sum_kernel, [((n, 128), bf16)] * NY)(keep, got)
    got = {i: shift(pieces[i], "y", NY, i) for i in (2, 1, 3)}
    return [pieces[0], got[1], got[2], got[3]]


def gather_y(part):
    got = {i: shift(part, "y", NY, i) for i in (2, 1, 3)}
    mine = [part, got[1], got[2], got[3]]
    return mine + [shift(m, "c", 2, 1) for m in mine]


def shards(grad_q_up, grad_kv_down, grad_kv_up):
    columns = NP * NZ
    factors = tuple(math.sqrt(g.shape[1] * columns) for g in (grad_q_up, grad_kv_down, grad_kv_up))
    flops = 2 * 4 * (QR * QR * QC + UR * UR * UC + DR * DR * 128)
    (packed,) = call(
        pack_kernel,
        [((XROWS, 128), bf16)],
        scratch=[pltpu.VMEM((DR, DC), bf16), pltpu.SemaphoreType.DMA((8,))],
        hbm=(0, 1, 2),
    )(grad_q_up, grad_kv_down, grad_kv_up)
    x = ring(packed)
    keep, send = call(
        functools.partial(gram_kernel, False), [((NY * DN, 128), bf16)] * 2, flops // 4
    )(x[0])
    (own,) = call(own_sum_kernel, [((DN, 128), bf16)])(*sum_y(keep, send, DN))
    n = PG - DN
    keep, send = call(
        functools.partial(gram_kernel, True), [((NY * n, 128), bf16)] * 2, flops // 2, after=(own,)
    )(*x[0:3])
    (total,) = call(y_sum_kernel, [((SENT, 128), bf16)])(own, *sum_y(keep, send, n))
    total = lax.all_to_all(total, "z", 0, 0, tiled=True)
    (total,) = call(z_sum_kernel, [((SENT, 128), bf16)])(total)
    total = lax.all_to_all(total, "z", 0, 0, tiled=True)
    left = shift(total[P_:S], "x", NX, 1)
    right = shift(total[C:PG], "x", NX, -1)
    (piece,) = call(join_kernel, [((PIECE, 128), bf16)])(total, left, right)
    gram, first_b, acc = call(
        first_kernel,
        [((GROWS, 128), bf16), ((XROWS, 128), bf16), ((XROWS, 128), f32)],
        flops,
    )(*gather_y(piece), *x)
    f = ring(first_b)
    (total,) = call(second_near_kernel, [((XROWS, 128), f32)], 3 * flops // 4)(gram, acc, *f[0:3])
    return tuple(
        call(
            functools.partial(second_far_kernel, factors),
            [((QR, QC), bf16), ((DR, DC), bf16), ((UR, UC), bf16)],
            flops // 4,
        )(gram, total, *f[3:5])
    )


def solution(mesh):
    fine = Mesh(mesh.devices.reshape(NY, NZ, 2, NX), ("y", "z", "c", "x"))
    placed = P("x", ("y", "z", "c"))
    return jax.shard_map(
        shards,
        mesh=fine,
        in_specs=(placed, placed, placed),
        out_specs=(placed, placed, placed),
        check_vma=False,
    )
```

```python
import functools
import math

import jax
import jax.numpy as jnp
from jax import lax
from jax.experimental import pallas as pl
from jax.experimental.pallas import tpu as pltpu
from jax.sharding import Mesh, PartitionSpec as P

coef_a = 3.4445
coef_b = -4.775
coef_c = 2.0315

bf16 = jnp.bfloat16
f32 = jnp.float32

QR, QC = 384, 384
DR, DC = 144, 112
UR, UC = 128, 512
NX, NY, NZ = 4, 4, 8
NP = 2 * NY

X1 = 2 * QR + DR
XROWS = X1 + QR + UR * (UC // 128)

QH, UH, DU = QR // 2, UR // 2, 80
DL = DR - DU

DN = 144
D, P_, C, S = 0, DN, DN + 96, DN + 192
PG = DN + 288
SHARD = 64
SENT = SHARD * NZ
HELD = (("D", DN), ("P", 96), ("S", 96), ("LP", 96), ("LC", 96), ("RC", 96), ("RS", 96))
PIECE = DN + 576
BASE = {name: NP * (DN * (i > 0) + 96 * max(i - 1, 0)) for i, (name, _) in enumerate(HELD)}
GROWS = NP * PIECE
DQ = (0, QR, 2 * QR - 128, 2 * QR)


def vmem(n):
    return [pl.BlockSpec(memory_space=pltpu.VMEM)] * n


def call(kernel, outs, flops=0, scratch=(), hbm=(), after=(), limit=40):
    def run(*args):
        n = len(args)
        args = (*args, *after)
        outs_t = tuple(jax.ShapeDtypeStruct(s, d) for s, d in outs)
        moved = sum(a.size * a.dtype.itemsize for a in args) + sum(
            s.size * s.dtype.itemsize for s in outs_t
        )
        return pl.pallas_call(
            skip(kernel, n, len(after)),
            out_shape=outs_t,
            in_specs=[
                pl.BlockSpec(memory_space=pltpu.HBM if i in hbm else pl.ANY if i >= n else pltpu.VMEM)
                for i in range(len(args))
            ],
            out_specs=tuple(vmem(len(outs))),
            scratch_shapes=list(scratch),
            cost_estimate=pl.CostEstimate(flops=flops, bytes_accessed=moved, transcendentals=0),
            compiler_params=pltpu.CompilerParams(vmem_limit_bytes=limit << 20),
        )(*args)

    return run


def skip(kernel, n, extra):
    return lambda *refs: kernel(*refs[:n], *refs[n + extra :])


def dot_t(a, b):
    return lax.dot_general(a, b, (((1,), (1,)), ((), ())), preferred_element_type=f32)


def dot(a, b):
    return jnp.dot(a, b, preferred_element_type=f32)


def lanes(parts):
    return jnp.concatenate(parts, axis=1)


def rows(parts):
    return jnp.concatenate(parts, axis=0)


def rows_of(block, lo, n):
    cut, parts = block
    if lo < cut:
        return parts[0][lo : lo + n, :]
    return parts[1][lo - cut : lo - cut + n, :]


def x_q(p):
    return lanes([rows_of(p, at, QR) for at in (0, QR, X1)])


def x_d(p):
    return rows_of(p, 2 * QR, DR)


def x_u(p):
    return lanes([rows_of(p, X1 + QR + UR * k, UR) for k in range(4)])


def dot_l(a, b):
    return lax.dot_general(a, b, (((0,), (0,)), ((), ())), preferred_element_type=f32)


def blocks_of(refs, cut):
    out = [(XROWS, (r,)) for r in refs[0:3]]
    return out + ([(cut, tuple(refs[3:5]))] if len(refs) == 5 else [])


def padded(v, to):
    return rows([v, jnp.zeros((to - v.shape[0], v.shape[1]), v.dtype)])


def pack_kernel(q, d, u, o, held, sems):
    moves = [(d, held)]
    for k in range(2):
        moves.append((q.at[:, 128 * k : 128 * (k + 1)], o.at[QR * k : QR * (k + 1), :]))
    moves.append((q.at[:, 256:384], o.at[X1 : X1 + QR, :]))
    for k in range(4):
        at = slice(X1 + QR + UR * k, X1 + QR + UR * (k + 1))
        moves.append((u.at[:, 128 * k : 128 * (k + 1)], o.at[at, :]))
    copies = [pltpu.make_async_copy(a, b, sems.at[i]) for i, (a, b) in enumerate(moves)]
    for copy in copies:
        copy.start()
    copies[0].wait()
    o[2 * QR : X1, :] = jnp.zeros((DR, 128), bf16)
    o[2 * QR : X1, 0:DC] = held[...]
    for copy in copies[1:]:
        copy.wait()


def half_products(a, b, upper):
    g = dot_t(x_q(a)[0:QH] if upper else x_q(a)[QH:QR], x_q(b))
    out = [(QH * k, g[:, 128 * k : 128 * (k + 1)]) for k in range(3)]
    at = 3 * QH
    out.append((at, dot_t(x_u(a)[0:UH] if upper else x_u(a)[UH:UR], x_u(b))))
    at += UH
    mine = x_d(a)[0:DU] if upper else x_d(a)[DU:DR]
    out.append((at, dot_t(mine, x_d(b)[0:128])))
    at += mine.shape[0]
    out.append((at, dot_t(x_d(b)[128:DR], padded(mine, 128))))
    at += DR - 128
    out.append((at, jnp.zeros((96 * NP - at, 128), f32)))
    return out


def gram_kernel(near, *refs):
    own = (XROWS, (refs[0],))
    left, right = ((XROWS, (r,)) for r in refs[1:3]) if near else (None, None)
    if near:
        keep, send = refs[-2:]
    else:
        keep, send, held = refs[-3:]
        held[...] = refs[0][...]
    total = PG - DN if near else DN

    def put(low, high, size, base, at, value):
        value = value.astype(bf16)
        done, n = 0, value.shape[0]
        while done < n:
            piece, off = divmod(at + done, size)
            m = min(n - done, size - off)
            ref = low if piece < NY else high
            to = (piece % NY) * total + base + off
            ref[to : to + m, :] = value[done : done + m, :]
            done += m

    def emit_own(low, high):
        g = dot_t(x_q(own), x_q(own))
        for k, at in enumerate(DQ):
            put(low, high, DN, D, at, g[128 * k : QR, 128 * k : 128 * (k + 1)])
        at = DQ[3]
        put(low, high, DN, D, at, dot_t(x_u(own), x_u(own)))
        g = dot_t(x_d(own), padded(x_d(own), 256))
        at += UR
        put(low, high, DN, D, at, g[:, 0:128])
        put(low, high, DN, D, at + DR, g[128:DR, 128:256])
        at += DR + DR - 128
        put(low, high, DN, D, at, jnp.zeros((DN * NP - at, 128), f32))

    def emit(low, high):
        if not near:
            emit_own(low, high)
            return
        for at, value in half_products(own, right, True):
            put(low, high, 96, P_ - DN, at, value)
        for at, value in half_products(left, own, False):
            put(low, high, 96, S - DN, at, value)

    def emit_cross(low, high, a, b, upper):
        for at, value in half_products(a, b, upper):
            put(low, high, 96, C - DN, at, value)

    core = lax.axis_index("c")
    first_two = lax.axis_index("x") < 2
    for mine, low, high in ((0, keep, send), (1, send, keep)):

        @pl.when(core == mine)
        def _():
            emit(low, high)

        if not near:
            continue

        @pl.when(jnp.logical_and(core == mine, first_two))
        def _():
            emit_cross(low, high, left, right, True)

        @pl.when(jnp.logical_and(core == mine, jnp.logical_not(first_two)))
        def _():
            emit_cross(low, high, right, left, False)


def core_sum_kernel(keep, got, *outs):
    y = lax.axis_index("y")
    n = outs[0].shape[0]
    for i, o in enumerate(outs):
        at = pl.ds(pl.multiple_of(lax.rem(y + i, NY) * n, 16), n)
        o[...] = (keep[at, :].astype(f32) + got[at, :].astype(f32)).astype(bf16)


def total_of(a, b, c, d):
    return (
        (a[...].astype(f32) + b[...].astype(f32)) + (c[...].astype(f32) + d[...].astype(f32))
    ).astype(bf16)


def own_sum_kernel(a, b, c, d, o):
    o[...] = total_of(a, b, c, d)


def y_sum_kernel(own, a, b, c, d, o):
    o[0:DN, :] = own[...]
    o[DN:PG, :] = total_of(a, b, c, d)
    o[PG:SENT, :] = jnp.zeros((SENT - PG, 128), bf16)


def z_sum_kernel(a, o):
    total = a[0:SHARD, :].astype(f32)
    for i in range(1, NZ):
        total = total + a[SHARD * i : SHARD * (i + 1), :].astype(f32)
    total = total.astype(bf16)
    for i in range(NZ):
        o[SHARD * i : SHARD * (i + 1), :] = total


def join_kernel(own, left, right, o):
    o[0:C, :] = own[0:C, :]
    o[C:S, :] = own[S:PG, :]
    o[S : S + 192, :] = left[...]
    o[S + 192 : PIECE, :] = right[...]


def unpack_gram(gram, mine, other):
    y, core = lax.axis_index("y"), lax.axis_index("c")
    for group, which in ((mine, core), (other, 1 - core)):
        for i, piece in enumerate(group):
            p = which * NY + lax.rem(y + NY - i, NY)
            at = 0
            for name, size in HELD:
                to = pl.multiple_of(BASE[name] + p * size, 16)
                gram[pl.ds(to, size), :] = piece[at : at + size, :]
                at += size


def half_q(gram, name):
    return lanes([gram[BASE[name] + QH * k : BASE[name] + QH * (k + 1), :] for k in range(3)])


def half_u(gram, name):
    at = BASE[name] + 3 * QH
    return gram[at : at + UH, :]


def half_d(gram, name, n):
    at = BASE[name] + 3 * QH + UH
    return gram[at : at + n, :], gram[at + n : at + n + DR - 128, :]


def straight(gram, upper, lower, b):
    q = dot(rows([half_q(gram, upper), half_q(gram, lower)]), x_q(b))
    u = dot(rows([half_u(gram, upper), half_u(gram, lower)]), x_u(b))
    main, rest = x_d(b)[0:128], x_d(b)[128:DR]
    parts = []
    for name, n in ((upper, DU), (lower, DL)):
        lead, last = half_d(gram, name, n)
        parts.append(dot(lead, main) + dot_l(last, rest)[0:n])
    return q, rows(parts), u


def turned(gram, upper, lower, b):
    q = dot_l(rows([half_q(gram, upper), half_q(gram, lower)]), x_q(b))
    u = dot_l(rows([half_u(gram, upper), half_u(gram, lower)]), x_u(b))
    d = None
    for name, n, v in ((upper, DU, x_d(b)[0:DU]), (lower, DL, x_d(b)[DU:DR])):
        lead, last = half_d(gram, name, n)
        term = rows([dot_l(lead, v), dot(last, padded(v, 128))])
        d = term if d is None else d + term
    return q, d, u


def own_product(gram, b):
    x = x_q(b)
    g0, g1, g2 = (gram[DQ[k] : DQ[k + 1], :] for k in range(3))
    q0, q1, q2 = (dot(g, x[128 * k : 128 * (k + 1)]) for k, g in enumerate((g0, g1, g2)))
    q = rows(
        [
            q0[0:128] + dot_l(g0[128:384], x[128:384]),
            q0[128:256] + q1[0:128] + dot_l(g1[128:256], x[256:384]),
            q0[256:384] + q1[128:256] + q2,
        ]
    )
    at = DQ[3]
    u = dot(gram[at : at + UR, :], x_u(b))
    at += UR
    lead, last = gram[at : at + DR, :], gram[at + DR : at + DR + DR - 128, :]
    main, rest = x_d(b)[0:128], x_d(b)[128:DR]
    side = rows([dot_l(lead[128:DR], rest), dot(last, padded(rest, 128))])
    return q, dot(lead, main) + side, u


def added(*terms):
    out = terms[0]
    for t in terms[1:]:
        out = tuple(a + b for a, b in zip(out, t))
    return out


def near_product(gram, own, left, right):
    return added(
        own_product(gram, own),
        straight(gram, "P", "RS", right),
        turned(gram, "LP", "S", left),
    )


def far_product(gram, block, use):
    x = lax.axis_index("x")
    outer = jnp.logical_or(x == 0, x == 3)

    @pl.when(outer)
    def _():
        use(straight(gram, "RC", "LC", block))

    @pl.when(jnp.logical_not(outer))
    def _():
        use(turned(gram, "LC", "RC", block))


def packed_parts(value):
    q, d, u = value
    out = [(at, q[:, 128 * k : 128 * (k + 1)]) for k, at in enumerate((0, QR, X1))]
    out.append((2 * QR, d))
    return out + [(X1 + QR + UR * k, u[:, 128 * k : 128 * (k + 1)]) for k in range(4)]


def first_kernel(*refs):
    own, left, right, far = blocks_of(refs[8:13], X1)
    gram, first_b, acc = refs[13:16]
    unpack_gram(gram, refs[0:4], refs[4:8])
    near = near_product(gram, own, left, right)

    def use(value):
        for at, v in packed_parts(added(near, value)):
            to = slice(at, at + v.shape[0])
            first_b[to, :] = v.astype(bf16)
            acc[to, :] = coef_a * refs[8][to, :].astype(f32) + coef_b * v

    far_product(gram, far, use)


def second_near_kernel(gram, acc, own, left, right, total):
    for at, v in packed_parts(near_product(gram, *blocks_of((own, left, right), 0))):
        to = slice(at, at + v.shape[0])
        total[to, :] = acc[to, :] + coef_c * v


def second_far_kernel(factors, gram, total, o1, o2, step_q, step_d, step_u):
    fq, fd, fu = factors

    def use(value):
        parts = packed_parts(value)
        done = [total[at : at + v.shape[0], :] + coef_c * v for at, v in parts]
        for k in range(3):
            step_q[:, 128 * k : 128 * (k + 1)] = (fq * done[k]).astype(bf16)
        step_d[...] = (fd * done[3]).astype(bf16)[:, 0:DC]
        for k in range(4):
            step_u[:, 128 * k : 128 * (k + 1)] = (fu * done[4 + k]).astype(bf16)

    far_product(gram, (X1, (o1, o2)), use)


def shift(value, axis, size, by):
    return lax.ppermute(value, axis, [(i, (i + by) % size) for i in range(size)])


def ring(own):
    left, right = shift(own, "x", NX, 1), shift(own, "x", NX, -1)
    return [own, left, right, shift(left[0:X1], "x", NX, 1), shift(right[X1:], "x", NX, -1)]


def sum_y(keep, send, n):
    got = shift(send, "c", 2, 1)
    pieces = call(core_sum_kernel, [((n, 128), bf16)] * NY)(keep, got)
    got = {i: shift(pieces[i], "y", NY, i) for i in (2, 1, 3)}
    return [pieces[0], got[1], got[2], got[3]]


def gather_y(part):
    got = {i: shift(part, "y", NY, i) for i in (2, 1, 3)}
    mine = [part, got[1], got[2], got[3]]
    return mine + [shift(m, "c", 2, 1) for m in mine]


def shards(grad_q_up, grad_kv_down, grad_kv_up):
    columns = NP * NZ
    factors = tuple(math.sqrt(g.shape[1] * columns) for g in (grad_q_up, grad_kv_down, grad_kv_up))
    flops = 2 * 4 * (QR * QR * QC + UR * UR * UC + DR * DR * 128)
    (packed,) = call(
        pack_kernel,
        [((XROWS, 128), bf16)],
        scratch=[pltpu.VMEM((DR, DC), bf16), pltpu.SemaphoreType.DMA((8,))],
        hbm=(0, 1, 2),
        limit=60,
    )(grad_q_up, grad_kv_down, grad_kv_up)
    x = ring(packed)
    keep, send, held = call(
        functools.partial(gram_kernel, False),
        [((NY * DN, 128), bf16)] * 2 + [((XROWS, 128), bf16)],
        flops // 4,
    )(x[0])
    x = [held] + x[1:]
    (own,) = call(own_sum_kernel, [((DN, 128), bf16)])(*sum_y(keep, send, DN))
    n = PG - DN
    keep, send = call(
        functools.partial(gram_kernel, True), [((NY * n, 128), bf16)] * 2, flops // 2, after=(own,)
    )(*x[0:3])
    (total,) = call(y_sum_kernel, [((SENT, 128), bf16)])(own, *sum_y(keep, send, n))
    total = lax.all_to_all(total, "z", 0, 0, tiled=True)
    (total,) = call(z_sum_kernel, [((SENT, 128), bf16)])(total)
    total = lax.all_to_all(total, "z", 0, 0, tiled=True)
    left = shift(total[P_:S], "x", NX, 1)
    right = shift(total[C:PG], "x", NX, -1)
    (piece,) = call(join_kernel, [((PIECE, 128), bf16)])(total, left, right)
    gram, first_b, acc = call(
        first_kernel,
        [((GROWS, 128), bf16), ((XROWS, 128), bf16), ((XROWS, 128), f32)],
        flops,
    )(*gather_y(piece), *x)
    f = ring(first_b)
    (total,) = call(second_near_kernel, [((XROWS, 128), f32)], 3 * flops // 4)(gram, acc, *f[0:3])
    return tuple(
        call(
            functools.partial(second_far_kernel, factors),
            [((QR, QC), bf16), ((DR, DC), bf16), ((UR, UC), bf16)],
            flops // 4,
        )(gram, total, *f[3:5])
    )


def solution(mesh):
    fine = Mesh(mesh.devices.reshape(NY, NZ, 2, NX), ("y", "z", "c", "x"))
    placed = P("x", ("y", "z", "c"))
    return jax.shard_map(
        shards,
        mesh=fine,
        in_specs=(placed, placed, placed),
        out_specs=(placed, placed, placed),
        check_vma=False,
    )
```

```python
import functools
import math

import jax
import jax.numpy as jnp
from jax import lax
from jax.experimental import pallas as pl
from jax.experimental.pallas import tpu as pltpu
from jax.sharding import Mesh, PartitionSpec as P

coef_a = 3.4445
coef_b = -4.775
coef_c = 2.0315

bf16 = jnp.bfloat16
f32 = jnp.float32

QR, QC = 384, 384
DR, DC = 144, 112
UR, UC = 128, 512
NX, NY, NZ = 4, 4, 8
NP = 2 * NY

X1 = 2 * QR + DR
XROWS = X1 + QR + UR * (UC // 128)

QH, UH, DU = QR // 2, UR // 2, 80
DL = DR - DU

DN = 144
D, P_, C, S = 0, DN, DN + 96, DN + 192
PG = DN + 288
SHARD = 64
SENT = SHARD * NZ
HELD = (("D", DN), ("P", 96), ("S", 96), ("LP", 96), ("LC", 96), ("RC", 96), ("RS", 96))
PIECE = DN + 576
BASE = {name: NP * (DN * (i > 0) + 96 * max(i - 1, 0)) for i, (name, _) in enumerate(HELD)}
GROWS = NP * PIECE
DQ = (0, QR, 2 * QR - 128, 2 * QR)


def vmem(n):
    return [pl.BlockSpec(memory_space=pltpu.VMEM)] * n


def call(kernel, outs, flops=0, scratch=(), hbm=(), after=(), limit=40):
    def run(*args):
        n = len(args)
        args = (*args, *after)
        outs_t = tuple(jax.ShapeDtypeStruct(s, d) for s, d in outs)
        moved = sum(a.size * a.dtype.itemsize for a in args) + sum(
            s.size * s.dtype.itemsize for s in outs_t
        )
        return pl.pallas_call(
            skip(kernel, n, len(after)),
            out_shape=outs_t,
            in_specs=[
                pl.BlockSpec(memory_space=pltpu.HBM if i in hbm else pl.ANY if i >= n else pltpu.VMEM)
                for i in range(len(args))
            ],
            out_specs=tuple(vmem(len(outs))),
            scratch_shapes=list(scratch),
            cost_estimate=pl.CostEstimate(flops=flops, bytes_accessed=moved, transcendentals=0),
            compiler_params=pltpu.CompilerParams(vmem_limit_bytes=limit << 20),
        )(*args)

    return run


def skip(kernel, n, extra):
    return lambda *refs: kernel(*refs[:n], *refs[n + extra :])


def dot_t(a, b):
    return lax.dot_general(a, b, (((1,), (1,)), ((), ())), preferred_element_type=f32)


def dot(a, b):
    return jnp.dot(a, b, preferred_element_type=f32)


def lanes(parts):
    return jnp.concatenate(parts, axis=1)


def rows(parts):
    return jnp.concatenate(parts, axis=0)


def rows_of(block, lo, n):
    cut, parts = block
    if lo < cut:
        return parts[0][lo : lo + n, :]
    return parts[1][lo - cut : lo - cut + n, :]


def x_q(p):
    return lanes([rows_of(p, at, QR) for at in (0, QR, X1)])


def x_d(p):
    return rows_of(p, 2 * QR, DR)


def x_u(p):
    return lanes([rows_of(p, X1 + QR + UR * k, UR) for k in range(4)])


def dot_l(a, b):
    return lax.dot_general(a, b, (((0,), (0,)), ((), ())), preferred_element_type=f32)


def blocks_of(refs, cut):
    out = [(XROWS, (r,)) for r in refs[0:3]]
    return out + ([(cut, tuple(refs[3:5]))] if len(refs) == 5 else [])


def padded(v, to):
    return rows([v, jnp.zeros((to - v.shape[0], v.shape[1]), v.dtype)])


def pack_kernel(q, d, u, o, held, sems):
    moves = [(d, held)]
    for k in range(2):
        moves.append((q.at[:, 128 * k : 128 * (k + 1)], o.at[QR * k : QR * (k + 1), :]))
    moves.append((q.at[:, 256:384], o.at[X1 : X1 + QR, :]))
    for k in range(4):
        at = slice(X1 + QR + UR * k, X1 + QR + UR * (k + 1))
        moves.append((u.at[:, 128 * k : 128 * (k + 1)], o.at[at, :]))
    copies = [pltpu.make_async_copy(a, b, sems.at[i]) for i, (a, b) in enumerate(moves)]
    for copy in copies:
        copy.start()
    copies[0].wait()
    o[2 * QR : X1, :] = jnp.zeros((DR, 128), bf16)
    o[2 * QR : X1, 0:DC] = held[...]
    for copy in copies[1:]:
        copy.wait()


def half_products(a, b, upper):
    g = dot_t(x_q(a)[0:QH] if upper else x_q(a)[QH:QR], x_q(b))
    out = [(QH * k, g[:, 128 * k : 128 * (k + 1)]) for k in range(3)]
    at = 3 * QH
    out.append((at, dot_t(x_u(a)[0:UH] if upper else x_u(a)[UH:UR], x_u(b))))
    at += UH
    mine = x_d(a)[0:DU] if upper else x_d(a)[DU:DR]
    out.append((at, dot_t(mine, x_d(b)[0:128])))
    at += mine.shape[0]
    out.append((at, dot_t(x_d(b)[128:DR], padded(mine, 128))))
    at += DR - 128
    out.append((at, jnp.zeros((96 * NP - at, 128), f32)))
    return out


def gram_kernel(near, *refs):
    own = (XROWS, (refs[0],))
    left, right = ((XROWS, (r,)) for r in refs[1:3]) if near else (None, None)
    if near:
        keep, send = refs[-2:]
    else:
        keep, send, held = refs[-3:]
        held[...] = refs[0][...]
    total = PG - DN if near else DN

    def put(low, high, size, base, at, value):
        value = value.astype(bf16)
        done, n = 0, value.shape[0]
        while done < n:
            piece, off = divmod(at + done, size)
            m = min(n - done, size - off)
            ref = low if piece < NY else high
            to = (piece % NY) * total + base + off
            ref[to : to + m, :] = value[done : done + m, :]
            done += m

    def emit_own(low, high):
        g = dot_t(x_q(own), x_q(own))
        for k, at in enumerate(DQ):
            put(low, high, DN, D, at, g[128 * k : QR, 128 * k : 128 * (k + 1)])
        at = DQ[3]
        put(low, high, DN, D, at, dot_t(x_u(own), x_u(own)))
        g = dot_t(x_d(own), padded(x_d(own), 256))
        at += UR
        put(low, high, DN, D, at, g[:, 0:128])
        put(low, high, DN, D, at + DR, g[128:DR, 128:256])
        at += DR + DR - 128
        put(low, high, DN, D, at, jnp.zeros((DN * NP - at, 128), f32))

    def emit(low, high):
        if not near:
            emit_own(low, high)
            return
        for at, value in half_products(own, right, True):
            put(low, high, 96, P_ - DN, at, value)
        for at, value in half_products(left, own, False):
            put(low, high, 96, S - DN, at, value)

    def emit_cross(low, high, a, b, upper):
        for at, value in half_products(a, b, upper):
            put(low, high, 96, C - DN, at, value)

    core = lax.axis_index("c")
    first_two = lax.axis_index("x") < 2
    for mine, low, high in ((0, keep, send), (1, send, keep)):

        @pl.when(core == mine)
        def _():
            emit(low, high)

        if not near:
            continue

        @pl.when(jnp.logical_and(core == mine, first_two))
        def _():
            emit_cross(low, high, left, right, True)

        @pl.when(jnp.logical_and(core == mine, jnp.logical_not(first_two)))
        def _():
            emit_cross(low, high, right, left, False)


def core_sum_kernel(keep, got, *outs):
    y = lax.axis_index("y")
    n = outs[0].shape[0]
    for i, o in enumerate(outs):
        at = pl.ds(pl.multiple_of(lax.rem(y + i, NY) * n, 16), n)
        o[...] = (keep[at, :].astype(f32) + got[at, :].astype(f32)).astype(bf16)


def total_of(a, b, c, d):
    return (
        (a[...].astype(f32) + b[...].astype(f32)) + (c[...].astype(f32) + d[...].astype(f32))
    ).astype(bf16)


def own_sum_kernel(a, b, c, d, o):
    o[...] = total_of(a, b, c, d)


def y_sum_kernel(own, a, b, c, d, o):
    o[0:DN, :] = own[...]
    o[DN:PG, :] = total_of(a, b, c, d)
    o[PG:SENT, :] = jnp.zeros((SENT - PG, 128), bf16)


def z_sum_kernel(a, o):
    total = a[0:SHARD, :].astype(f32)
    for i in range(1, NZ):
        total = total + a[SHARD * i : SHARD * (i + 1), :].astype(f32)
    total = total.astype(bf16)
    for i in range(NZ):
        o[SHARD * i : SHARD * (i + 1), :] = total


def join_kernel(own, left, right, o):
    o[0:C, :] = own[0:C, :]
    o[C:S, :] = own[S:PG, :]
    o[S : S + 192, :] = left[...]
    o[S + 192 : PIECE, :] = right[...]


def unpack_gram(gram, mine, other):
    y, core = lax.axis_index("y"), lax.axis_index("c")
    for group, which in ((mine, core), (other, 1 - core)):
        for i, piece in enumerate(group):
            p = which * NY + lax.rem(y + NY - i, NY)
            at = 0
            for name, size in HELD:
                to = pl.multiple_of(BASE[name] + p * size, 16)
                gram[pl.ds(to, size), :] = piece[at : at + size, :]
                at += size


def half_q(gram, name):
    return lanes([gram[BASE[name] + QH * k : BASE[name] + QH * (k + 1), :] for k in range(3)])


def half_u(gram, name):
    at = BASE[name] + 3 * QH
    return gram[at : at + UH, :]


def half_d(gram, name, n):
    at = BASE[name] + 3 * QH + UH
    return gram[at : at + n, :], gram[at + n : at + n + DR - 128, :]


def straight(gram, upper, lower, b):
    q = dot(rows([half_q(gram, upper), half_q(gram, lower)]), x_q(b))
    u = dot(rows([half_u(gram, upper), half_u(gram, lower)]), x_u(b))
    main, rest = x_d(b)[0:128], x_d(b)[128:DR]
    parts = []
    for name, n in ((upper, DU), (lower, DL)):
        lead, last = half_d(gram, name, n)
        parts.append(dot(lead, main) + dot_l(last, rest)[0:n])
    return q, rows(parts), u


def turned(gram, upper, lower, b):
    q = dot_l(rows([half_q(gram, upper), half_q(gram, lower)]), x_q(b))
    u = dot_l(rows([half_u(gram, upper), half_u(gram, lower)]), x_u(b))
    d = None
    for name, n, v in ((upper, DU, x_d(b)[0:DU]), (lower, DL, x_d(b)[DU:DR])):
        lead, last = half_d(gram, name, n)
        term = rows([dot_l(lead, v), dot(last, padded(v, 128))])
        d = term if d is None else d + term
    return q, d, u


def own_product(gram, b):
    x = x_q(b)
    g0, g1, g2 = (gram[DQ[k] : DQ[k + 1], :] for k in range(3))
    q0, q1, q2 = (dot(g, x[128 * k : 128 * (k + 1)]) for k, g in enumerate((g0, g1, g2)))
    q = rows(
        [
            q0[0:128] + dot_l(g0[128:384], x[128:384]),
            q0[128:256] + q1[0:128] + dot_l(g1[128:256], x[256:384]),
            q0[256:384] + q1[128:256] + q2,
        ]
    )
    at = DQ[3]
    u = dot(gram[at : at + UR, :], x_u(b))
    at += UR
    lead, last = gram[at : at + DR, :], gram[at + DR : at + DR + DR - 128, :]
    main, rest = x_d(b)[0:128], x_d(b)[128:DR]
    side = rows([dot_l(lead[128:DR], rest), dot(last, padded(rest, 128))])
    return q, dot(lead, main) + side, u


def added(*terms):
    out = terms[0]
    for t in terms[1:]:
        out = tuple(a + b for a, b in zip(out, t))
    return out


def near_product(gram, own, left, right):
    return added(
        own_product(gram, own),
        straight(gram, "P", "RS", right),
        turned(gram, "LP", "S", left),
    )


def far_product(gram, block, use):
    x = lax.axis_index("x")
    outer = jnp.logical_or(x == 0, x == 3)

    @pl.when(outer)
    def _():
        use(straight(gram, "RC", "LC", block))

    @pl.when(jnp.logical_not(outer))
    def _():
        use(turned(gram, "LC", "RC", block))


def packed_parts(value):
    q, d, u = value
    out = [(at, q[:, 128 * k : 128 * (k + 1)]) for k, at in enumerate((0, QR, X1))]
    out.append((2 * QR, d))
    return out + [(X1 + QR + UR * k, u[:, 128 * k : 128 * (k + 1)]) for k in range(4)]


def first_kernel(*refs):
    own, left, right, far = blocks_of(refs[8:13], X1)
    gram, first_b, acc = refs[13:16]
    unpack_gram(gram, refs[0:4], refs[4:8])
    near = near_product(gram, own, left, right)

    def use(value):
        for at, v in packed_parts(added(near, value)):
            to = slice(at, at + v.shape[0])
            first_b[to, :] = v.astype(bf16)
            acc[to, :] = v

    far_product(gram, far, use)


def second_near_kernel(gram, acc, x, own, left, right, total):
    for at, v in packed_parts(near_product(gram, *blocks_of((own, left, right), 0))):
        to = slice(at, at + v.shape[0])
        total[to, :] = (coef_a * x[to, :].astype(f32) + coef_b * acc[to, :]) + coef_c * v


def second_far_kernel(factors, gram, total, o1, o2, step_q, step_d, step_u):
    fq, fd, fu = factors

    def use(value):
        parts = packed_parts(value)
        done = [total[at : at + v.shape[0], :] + coef_c * v for at, v in parts]
        for k in range(3):
            step_q[:, 128 * k : 128 * (k + 1)] = (fq * done[k]).astype(bf16)
        step_d[...] = (fd * done[3]).astype(bf16)[:, 0:DC]
        for k in range(4):
            step_u[:, 128 * k : 128 * (k + 1)] = (fu * done[4 + k]).astype(bf16)

    far_product(gram, (X1, (o1, o2)), use)


def shift(value, axis, size, by):
    return lax.ppermute(value, axis, [(i, (i + by) % size) for i in range(size)])


def ring(own):
    left, right = shift(own, "x", NX, 1), shift(own, "x", NX, -1)
    return [own, left, right, shift(left[0:X1], "x", NX, 1), shift(right[X1:], "x", NX, -1)]


def sum_y(keep, send, n):
    got = shift(send, "c", 2, 1)
    pieces = call(core_sum_kernel, [((n, 128), bf16)] * NY)(keep, got)
    got = {i: shift(pieces[i], "y", NY, i) for i in (2, 1, 3)}
    return [pieces[0], got[1], got[2], got[3]]


def gather_y(part):
    got = {i: shift(part, "y", NY, i) for i in (2, 1, 3)}
    mine = [part, got[1], got[2], got[3]]
    return mine + [shift(m, "c", 2, 1) for m in mine]


def shards(grad_q_up, grad_kv_down, grad_kv_up):
    columns = NP * NZ
    factors = tuple(math.sqrt(g.shape[1] * columns) for g in (grad_q_up, grad_kv_down, grad_kv_up))
    flops = 2 * 4 * (QR * QR * QC + UR * UR * UC + DR * DR * 128)
    (packed,) = call(
        pack_kernel,
        [((XROWS, 128), bf16)],
        scratch=[pltpu.VMEM((DR, DC), bf16), pltpu.SemaphoreType.DMA((8,))],
        hbm=(0, 1, 2),
        limit=60,
    )(grad_q_up, grad_kv_down, grad_kv_up)
    x = ring(packed)
    keep, send, held = call(
        functools.partial(gram_kernel, False),
        [((NY * DN, 128), bf16)] * 2 + [((XROWS, 128), bf16)],
        flops // 4,
    )(x[0])
    x = [held] + x[1:]
    (own,) = call(own_sum_kernel, [((DN, 128), bf16)])(*sum_y(keep, send, DN))
    n = PG - DN
    keep, send = call(
        functools.partial(gram_kernel, True), [((NY * n, 128), bf16)] * 2, flops // 2, after=(own,)
    )(*x[0:3])
    (total,) = call(y_sum_kernel, [((SENT, 128), bf16)])(own, *sum_y(keep, send, n))
    total = lax.all_to_all(total, "z", 0, 0, tiled=True)
    (total,) = call(z_sum_kernel, [((SENT, 128), bf16)])(total)
    total = lax.all_to_all(total, "z", 0, 0, tiled=True)
    left = shift(total[P_:S], "x", NX, 1)
    right = shift(total[C:PG], "x", NX, -1)
    (piece,) = call(join_kernel, [((PIECE, 128), bf16)])(total, left, right)
    gram, first_b, acc = call(
        first_kernel,
        [((GROWS, 128), bf16), ((XROWS, 128), bf16), ((XROWS, 128), f32)],
        flops,
    )(*gather_y(piece), *x)
    f = ring(first_b)
    (total,) = call(second_near_kernel, [((XROWS, 128), f32)], 3 * flops // 4)(
        gram, acc, x[0], *f[0:3]
    )
    return tuple(
        call(
            functools.partial(second_far_kernel, factors),
            [((QR, QC), bf16), ((DR, DC), bf16), ((UR, UC), bf16)],
            flops // 4,
        )(gram, total, *f[3:5])
    )


def solution(mesh):
    fine = Mesh(mesh.devices.reshape(NY, NZ, 2, NX), ("y", "z", "c", "x"))
    placed = P("x", ("y", "z", "c"))
    return jax.shard_map(
        shards,
        mesh=fine,
        in_specs=(placed, placed, placed),
        out_specs=(placed, placed, placed),
        check_vma=False,
    )
```

```python
import functools
import math

import jax
import jax.numpy as jnp
from jax import lax
from jax.experimental import pallas as pl
from jax.experimental.pallas import tpu as pltpu
from jax.sharding import Mesh, PartitionSpec as P

coef_a = 3.4445
coef_b = -4.775
coef_c = 2.0315

bf16 = jnp.bfloat16
f32 = jnp.float32

QR, QC = 384, 384
DR, DC = 144, 112
UR, UC = 128, 512
NX, NY, NZ = 4, 4, 8
NP = 2 * NY

X1 = 2 * QR + DR
XROWS = X1 + QR + UR * (UC // 128)

QH, UH, DU = QR // 2, UR // 2, 80
DL = DR - DU

DN = 144
D, P_, C, S = 0, DN, DN + 96, DN + 192
PG = DN + 288
SHARD = 64
SENT = SHARD * NZ
HELD = (("D", DN), ("P", 96), ("S", 96), ("LP", 96), ("LC", 96), ("RC", 96), ("RS", 96))
PIECE = DN + 576
BASE = {name: NP * (DN * (i > 0) + 96 * max(i - 1, 0)) for i, (name, _) in enumerate(HELD)}
GROWS = NP * PIECE
DQ = (0, QR, 2 * QR - 128, 2 * QR)


def vmem(n):
    return [pl.BlockSpec(memory_space=pltpu.VMEM)] * n


def call(kernel, outs, flops=0, scratch=(), hbm=(), after=(), limit=40, out_hbm=False):
    def run(*args):
        n = len(args)
        args = (*args, *after)
        outs_t = tuple(jax.ShapeDtypeStruct(s, d) for s, d in outs)
        moved = sum(a.size * a.dtype.itemsize for a in args) + sum(
            s.size * s.dtype.itemsize for s in outs_t
        )
        return pl.pallas_call(
            skip(kernel, n, len(after)),
            out_shape=outs_t,
            in_specs=[
                pl.BlockSpec(memory_space=pltpu.HBM if i in hbm else pl.ANY if i >= n else pltpu.VMEM)
                for i in range(len(args))
            ],
            out_specs=tuple(
                [pl.BlockSpec(memory_space=pl.ANY)] * len(outs) if out_hbm else vmem(len(outs))
            ),
            scratch_shapes=list(scratch),
            cost_estimate=pl.CostEstimate(flops=flops, bytes_accessed=moved, transcendentals=0),
            compiler_params=pltpu.CompilerParams(vmem_limit_bytes=limit << 20),
        )(*args)

    return run


def skip(kernel, n, extra):
    return lambda *refs: kernel(*refs[:n], *refs[n + extra :])


def dot_t(a, b):
    return lax.dot_general(a, b, (((1,), (1,)), ((), ())), preferred_element_type=f32)


def dot(a, b):
    return jnp.dot(a, b, preferred_element_type=f32)


def lanes(parts):
    return jnp.concatenate(parts, axis=1)


def rows(parts):
    return jnp.concatenate(parts, axis=0)


def rows_of(block, lo, n):
    cut, parts = block
    if lo < cut:
        return parts[0][lo : lo + n, :]
    return parts[1][lo - cut : lo - cut + n, :]


def x_q(p):
    return lanes([rows_of(p, at, QR) for at in (0, QR, X1)])


def x_d(p):
    return rows_of(p, 2 * QR, DR)


def x_u(p):
    return lanes([rows_of(p, X1 + QR + UR * k, UR) for k in range(4)])


def dot_l(a, b):
    return lax.dot_general(a, b, (((0,), (0,)), ((), ())), preferred_element_type=f32)


def blocks_of(refs, cut):
    out = [(XROWS, (r,)) for r in refs[0:3]]
    return out + ([(cut, tuple(refs[3:5]))] if len(refs) == 5 else [])


def padded(v, to):
    return rows([v, jnp.zeros((to - v.shape[0], v.shape[1]), v.dtype)])


def pack_kernel(q, d, u, o, held, sems):
    moves = [(d, held)]
    for k in range(2):
        moves.append((q.at[:, 128 * k : 128 * (k + 1)], o.at[QR * k : QR * (k + 1), :]))
    moves.append((q.at[:, 256:384], o.at[X1 : X1 + QR, :]))
    for k in range(4):
        at = slice(X1 + QR + UR * k, X1 + QR + UR * (k + 1))
        moves.append((u.at[:, 128 * k : 128 * (k + 1)], o.at[at, :]))
    copies = [pltpu.make_async_copy(a, b, sems.at[i]) for i, (a, b) in enumerate(moves)]
    for copy in copies:
        copy.start()
    copies[0].wait()
    o[2 * QR : X1, :] = jnp.zeros((DR, 128), bf16)
    o[2 * QR : X1, 0:DC] = held[...]
    for copy in copies[1:]:
        copy.wait()


def half_products(a, b, upper):
    g = dot_t(x_q(a)[0:QH] if upper else x_q(a)[QH:QR], x_q(b))
    out = [(QH * k, g[:, 128 * k : 128 * (k + 1)]) for k in range(3)]
    at = 3 * QH
    out.append((at, dot_t(x_u(a)[0:UH] if upper else x_u(a)[UH:UR], x_u(b))))
    at += UH
    mine = x_d(a)[0:DU] if upper else x_d(a)[DU:DR]
    out.append((at, dot_t(mine, x_d(b)[0:128])))
    at += mine.shape[0]
    out.append((at, dot_t(x_d(b)[128:DR], padded(mine, 128))))
    at += DR - 128
    out.append((at, jnp.zeros((96 * NP - at, 128), f32)))
    return out


def gram_kernel(near, *refs):
    own = (XROWS, (refs[0],))
    left, right = ((XROWS, (r,)) for r in refs[1:3]) if near else (None, None)
    if near:
        keep, send = refs[-2:]
    else:
        keep, send, held = refs[-3:]
        held[...] = refs[0][...]
    total = PG - DN if near else DN

    def put(low, high, size, base, at, value):
        value = value.astype(bf16)
        done, n = 0, value.shape[0]
        while done < n:
            piece, off = divmod(at + done, size)
            m = min(n - done, size - off)
            ref = low if piece < NY else high
            to = (piece % NY) * total + base + off
            ref[to : to + m, :] = value[done : done + m, :]
            done += m

    def emit_own(low, high):
        g = dot_t(x_q(own), x_q(own))
        for k, at in enumerate(DQ):
            put(low, high, DN, D, at, g[128 * k : QR, 128 * k : 128 * (k + 1)])
        at = DQ[3]
        put(low, high, DN, D, at, dot_t(x_u(own), x_u(own)))
        g = dot_t(x_d(own), padded(x_d(own), 256))
        at += UR
        put(low, high, DN, D, at, g[:, 0:128])
        put(low, high, DN, D, at + DR, g[128:DR, 128:256])
        at += DR + DR - 128
        put(low, high, DN, D, at, jnp.zeros((DN * NP - at, 128), f32))

    def emit(low, high):
        if not near:
            emit_own(low, high)
            return
        for at, value in half_products(own, right, True):
            put(low, high, 96, P_ - DN, at, value)
        for at, value in half_products(left, own, False):
            put(low, high, 96, S - DN, at, value)

    def emit_cross(low, high, a, b, upper):
        for at, value in half_products(a, b, upper):
            put(low, high, 96, C - DN, at, value)

    core = lax.axis_index("c")
    first_two = lax.axis_index("x") < 2
    for mine, low, high in ((0, keep, send), (1, send, keep)):

        @pl.when(core == mine)
        def _():
            emit(low, high)

        if not near:
            continue

        @pl.when(jnp.logical_and(core == mine, first_two))
        def _():
            emit_cross(low, high, left, right, True)

        @pl.when(jnp.logical_and(core == mine, jnp.logical_not(first_two)))
        def _():
            emit_cross(low, high, right, left, False)


def core_sum_kernel(keep, got, *outs):
    y = lax.axis_index("y")
    n = outs[0].shape[0]
    for i, o in enumerate(outs):
        at = pl.ds(pl.multiple_of(lax.rem(y + i, NY) * n, 16), n)
        o[...] = (keep[at, :].astype(f32) + got[at, :].astype(f32)).astype(bf16)


def total_of(a, b, c, d):
    return (
        (a[...].astype(f32) + b[...].astype(f32)) + (c[...].astype(f32) + d[...].astype(f32))
    ).astype(bf16)


def own_sum_kernel(a, b, c, d, o):
    o[...] = total_of(a, b, c, d)


def y_sum_kernel(own, a, b, c, d, o):
    o[0:DN, :] = own[...]
    o[DN:PG, :] = total_of(a, b, c, d)
    o[PG:SENT, :] = jnp.zeros((SENT - PG, 128), bf16)


def z_sum_kernel(a, o):
    total = a[0:SHARD, :].astype(f32)
    for i in range(1, NZ):
        total = total + a[SHARD * i : SHARD * (i + 1), :].astype(f32)
    total = total.astype(bf16)
    for i in range(NZ):
        o[SHARD * i : SHARD * (i + 1), :] = total


def join_kernel(own, left, right, o):
    o[0:C, :] = own[0:C, :]
    o[C:S, :] = own[S:PG, :]
    o[S : S + 192, :] = left[...]
    o[S + 192 : PIECE, :] = right[...]


def unpack_gram(gram, mine, other):
    y, core = lax.axis_index("y"), lax.axis_index("c")
    for group, which in ((mine, core), (other, 1 - core)):
        for i, piece in enumerate(group):
            p = which * NY + lax.rem(y + NY - i, NY)
            at = 0
            for name, size in HELD:
                to = pl.multiple_of(BASE[name] + p * size, 16)
                gram[pl.ds(to, size), :] = piece[at : at + size, :]
                at += size


def half_q(gram, name):
    return lanes([gram[BASE[name] + QH * k : BASE[name] + QH * (k + 1), :] for k in range(3)])


def half_u(gram, name):
    at = BASE[name] + 3 * QH
    return gram[at : at + UH, :]


def half_d(gram, name, n):
    at = BASE[name] + 3 * QH + UH
    return gram[at : at + n, :], gram[at + n : at + n + DR - 128, :]


def straight(gram, upper, lower, b):
    q = dot(rows([half_q(gram, upper), half_q(gram, lower)]), x_q(b))
    u = dot(rows([half_u(gram, upper), half_u(gram, lower)]), x_u(b))
    main, rest = x_d(b)[0:128], x_d(b)[128:DR]
    parts = []
    for name, n in ((upper, DU), (lower, DL)):
        lead, last = half_d(gram, name, n)
        parts.append(dot(lead, main) + dot_l(last, rest)[0:n])
    return q, rows(parts), u


def turned(gram, upper, lower, b):
    q = dot_l(rows([half_q(gram, upper), half_q(gram, lower)]), x_q(b))
    u = dot_l(rows([half_u(gram, upper), half_u(gram, lower)]), x_u(b))
    d = None
    for name, n, v in ((upper, DU, x_d(b)[0:DU]), (lower, DL, x_d(b)[DU:DR])):
        lead, last = half_d(gram, name, n)
        term = rows([dot_l(lead, v), dot(last, padded(v, 128))])
        d = term if d is None else d + term
    return q, d, u


def own_product(gram, b):
    x = x_q(b)
    g0, g1, g2 = (gram[DQ[k] : DQ[k + 1], :] for k in range(3))
    q0, q1, q2 = (dot(g, x[128 * k : 128 * (k + 1)]) for k, g in enumerate((g0, g1, g2)))
    q = rows(
        [
            q0[0:128] + dot_l(g0[128:384], x[128:384]),
            q0[128:256] + q1[0:128] + dot_l(g1[128:256], x[256:384]),
            q0[256:384] + q1[128:256] + q2,
        ]
    )
    at = DQ[3]
    u = dot(gram[at : at + UR, :], x_u(b))
    at += UR
    lead, last = gram[at : at + DR, :], gram[at + DR : at + DR + DR - 128, :]
    main, rest = x_d(b)[0:128], x_d(b)[128:DR]
    side = rows([dot_l(lead[128:DR], rest), dot(last, padded(rest, 128))])
    return q, dot(lead, main) + side, u


def added(*terms):
    out = terms[0]
    for t in terms[1:]:
        out = tuple(a + b for a, b in zip(out, t))
    return out


def near_product(gram, own, left, right):
    return added(
        own_product(gram, own),
        straight(gram, "P", "RS", right),
        turned(gram, "LP", "S", left),
    )


def far_product(gram, block, use):
    x = lax.axis_index("x")
    outer = jnp.logical_or(x == 0, x == 3)

    @pl.when(outer)
    def _():
        use(straight(gram, "RC", "LC", block))

    @pl.when(jnp.logical_not(outer))
    def _():
        use(turned(gram, "LC", "RC", block))


def packed_parts(value):
    q, d, u = value
    out = [(at, q[:, 128 * k : 128 * (k + 1)]) for k, at in enumerate((0, QR, X1))]
    out.append((2 * QR, d))
    return out + [(X1 + QR + UR * k, u[:, 128 * k : 128 * (k + 1)]) for k in range(4)]


def first_kernel(*refs):
    own, left, right, far = blocks_of(refs[8:13], X1)
    gram, first_b, acc = refs[13:16]
    unpack_gram(gram, refs[0:4], refs[4:8])
    near = near_product(gram, own, left, right)

    def use(value):
        for at, v in packed_parts(added(near, value)):
            to = slice(at, at + v.shape[0])
            first_b[to, :] = v.astype(bf16)
            acc[to, :] = v

    far_product(gram, far, use)


def second_near_kernel(gram, acc, x, own, left, right, total):
    for at, v in packed_parts(near_product(gram, *blocks_of((own, left, right), 0))):
        to = slice(at, at + v.shape[0])
        total[to, :] = (coef_a * x[to, :].astype(f32) + coef_b * acc[to, :]) + coef_c * v


def second_far_kernel(factors, gram, total, o1, o2, out_q, out_d, out_u, *scratch):
    fq, fd, fu = factors
    step_q, step_d, step_u, sems = scratch
    moves = [(step_q.at[:, 128 * k : 128 * (k + 1)], out_q.at[:, 128 * k : 128 * (k + 1)]) for k in range(3)]
    moves += [(step_d, out_d), (step_u, out_u)]
    copies = [pltpu.make_async_copy(a, b, sems.at[i]) for i, (a, b) in enumerate(moves)]

    def use(value):
        parts = packed_parts(value)
        done = [total[at : at + v.shape[0], :] + coef_c * v for at, v in parts]
        for k in range(3):
            step_q[:, 128 * k : 128 * (k + 1)] = (fq * done[k]).astype(bf16)
            copies[k].start()
        step_d[...] = (fd * done[3]).astype(bf16)[:, 0:DC]
        copies[3].start()
        for k in range(4):
            step_u[:, 128 * k : 128 * (k + 1)] = (fu * done[4 + k]).astype(bf16)
        copies[4].start()
        for copy in copies:
            copy.wait()

    far_product(gram, (X1, (o1, o2)), use)


def shift(value, axis, size, by):
    return lax.ppermute(value, axis, [(i, (i + by) % size) for i in range(size)])


def ring(own):
    left, right = shift(own, "x", NX, 1), shift(own, "x", NX, -1)
    return [own, left, right, shift(left[0:X1], "x", NX, 1), shift(right[X1:], "x", NX, -1)]


def sum_y(keep, send, n):
    got = shift(send, "c", 2, 1)
    pieces = call(core_sum_kernel, [((n, 128), bf16)] * NY)(keep, got)
    got = {i: shift(pieces[i], "y", NY, i) for i in (2, 1, 3)}
    return [pieces[0], got[1], got[2], got[3]]


def gather_y(part):
    got = {i: shift(part, "y", NY, i) for i in (2, 1, 3)}
    mine = [part, got[1], got[2], got[3]]
    return mine + [shift(m, "c", 2, 1) for m in mine]


def shards(grad_q_up, grad_kv_down, grad_kv_up):
    columns = NP * NZ
    factors = tuple(math.sqrt(g.shape[1] * columns) for g in (grad_q_up, grad_kv_down, grad_kv_up))
    flops = 2 * 4 * (QR * QR * QC + UR * UR * UC + DR * DR * 128)
    (packed,) = call(
        pack_kernel,
        [((XROWS, 128), bf16)],
        scratch=[pltpu.VMEM((DR, DC), bf16), pltpu.SemaphoreType.DMA((8,))],
        hbm=(0, 1, 2),
        limit=60,
    )(grad_q_up, grad_kv_down, grad_kv_up)
    x = ring(packed)
    keep, send, held = call(
        functools.partial(gram_kernel, False),
        [((NY * DN, 128), bf16)] * 2 + [((XROWS, 128), bf16)],
        flops // 4,
    )(x[0])
    x = [held] + x[1:]
    (own,) = call(own_sum_kernel, [((DN, 128), bf16)])(*sum_y(keep, send, DN))
    n = PG - DN
    keep, send = call(
        functools.partial(gram_kernel, True), [((NY * n, 128), bf16)] * 2, flops // 2, after=(own,)
    )(*x[0:3])
    (total,) = call(y_sum_kernel, [((SENT, 128), bf16)])(own, *sum_y(keep, send, n))
    total = lax.all_to_all(total, "z", 0, 0, tiled=True)
    (total,) = call(z_sum_kernel, [((SENT, 128), bf16)])(total)
    total = lax.all_to_all(total, "z", 0, 0, tiled=True)
    left = shift(total[P_:S], "x", NX, 1)
    right = shift(total[C:PG], "x", NX, -1)
    (piece,) = call(join_kernel, [((PIECE, 128), bf16)])(total, left, right)
    gram, first_b, acc = call(
        first_kernel,
        [((GROWS, 128), bf16), ((XROWS, 128), bf16), ((XROWS, 128), f32)],
        flops,
    )(*gather_y(piece), *x)
    f = ring(first_b)
    (total,) = call(second_near_kernel, [((XROWS, 128), f32)], 3 * flops // 4)(
        gram, acc, x[0], *f[0:3]
    )
    return tuple(
        call(
            functools.partial(second_far_kernel, factors),
            [((QR, QC), bf16), ((DR, DC), bf16), ((UR, UC), bf16)],
            flops // 4,
            scratch=[
                pltpu.VMEM((QR, QC), bf16),
                pltpu.VMEM((DR, DC), bf16),
                pltpu.VMEM((UR, UC), bf16),
                pltpu.SemaphoreType.DMA((5,)),
            ],
            out_hbm=True,
        )(gram, total, *f[3:5])
    )


def solution(mesh):
    fine = Mesh(mesh.devices.reshape(NY, NZ, 2, NX), ("y", "z", "c", "x"))
    placed = P("x", ("y", "z", "c"))
    return jax.shard_map(
        shards,
        mesh=fine,
        in_specs=(placed, placed, placed),
        out_specs=(placed, placed, placed),
        check_vma=False,
    )
```
